32 devices in a mesh: phase: 4 (over y, x), ctx: 8 (over z, core).
Axes of the slice: x: 2, y: 2, z: 4, core: 2. Of those that a mesh axis runs over, the one named last changes fastest.
Arguments:
- hidden: bfloat16 [4, 1024, 4096], P('phase', 'ctx'), may hold values from -6 to 6
- queries: bfloat16 [4, 1024, 2048], P('phase', 'ctx'), may hold values from -400 to 400
- key_value_weight: bfloat16 [4, 4096, 1024], P('phase'), may hold values from -0.09375 to 0.09375
- doc_ids: int32 [4, 1024], P('phase'), may hold values from 0 to 7, never falling along the last dimension, each value on 1 to 768 neighbouring positions
- scored: int32 [4, 1024], P('phase', 'ctx'), may hold values 0 or 1
Outputs:
- passed: bfloat16 [4, 1024, 2048], P('phase', 'ctx')
The draws below stay inside these ranges and needn't reach their ends.
Inputs may be any that keep to these rules, and one draw needn't show every extreme that they name: doc_ids never fall along a sequence; one document spans exactly 768 tokens.
All inputs are finite; a program needn't handle non-finite values. No bound on the sum of `scored` on one device may be relied on, other than what follows from the above.
Results may differ from the reference program's by a relative error of at most 0.008.
The reference program's roundings to bfloat16 on the way count: a program that leaves them out, or rounds other values in their place, can miss the bound.
Values may be sent and summed in bfloat16 or wider, within the bound.
No kernel may reach another device: no remote copies, remote signals or barrier semaphores. Data moves between devices by JAX's collectives and lax.ppermute only.
A program may use at most 128 MiB of HBM per device.

```python
import math
import jax
import jax.numpy as jnp
import numpy as np
from jax import lax

MODEL_WIDTH = 4096
QUERY_HEADS = 16
KEY_VALUE_HEADS = 4
HEAD_SIZE = 128
DOCS = 8
RELAY_SECTIONS = 4
SEQUENCE_TOKENS = 1024


def draw_queries(key, part):
    base = jnp.clip(jax.random.normal(key, (RELAY_SECTIONS, SEQUENCE_TOKENS, QUERY_HEADS * HEAD_SIZE), jnp.float32), -6.0, 6.0)
    return base.astype(jnp.bfloat16)


def plant(entries, own_key, low, largest):
    shape = entries.shape
    spot = [jax.random.randint(jax.random.fold_in(own_key, axis), (), 0, shape[axis]) for axis in range(len(shape))]
    entries = entries.at[tuple(spot)].set(low)
    longest = shape.index(max(shape))
    spot[longest] = (spot[longest] + 1) % shape[longest]
    return entries.at[tuple(spot)].set(largest)


def levels(rng, extent, pieces, low, high):
    def one(axis_at, parts):
        draws = jax.random.uniform(jax.random.fold_in(jax.random.fold_in(rng, 6), axis_at), (parts,), jnp.float32, low / len(pieces), high / len(pieces))
        return jnp.repeat(jnp.exp(draws), extent[axis_at] // parts).reshape((-1,) + (1,) * (len(extent) - axis_at - 1))

    level = one(*pieces[0])
    for cut in pieces[1:]:
        level = level * one(*cut)
    return level


def profile(count, total, limit, slope):
    portions = [(1 << 20) // math.isqrt(rank ** slope) + 1 for rank in range(2, count + 1)]
    spare, holding = total - limit - (count - 1), [1] * (count - 1)
    while spare > 0:
        free = [i for i in range(count - 1) if holding[i] < limit]
        mass, left = sum([portions[i] for i in free]), spare
        for i in free:
            extra = min(limit - holding[i], max(1, left * portions[i] // mass), spare)
            holding[i] = holding[i] + extra
            spare = spare - extra
    return np.array([limit] + holding)


def ragged(own_key, count, total, limit, slope):
    if count == 2:
        one = jax.random.randint(own_key, (), max(1, total - limit), min(limit, total - 1) + 1)
        return jnp.stack([one, total - one])
    tallies = jnp.asarray(profile(count, total, limit, slope), jnp.int32)
    pairs = (count - 1) // 2
    donor, taker = tallies[1:1 + 2 * pairs:2], tallies[2:2 + 2 * pairs:2]
    room = jnp.minimum(donor - 1, limit - taker)
    moved = jax.random.randint(jax.random.fold_in(own_key, 1), (pairs,), 0, 1 << 20) % (room + 1)
    tallies = tallies.at[1:1 + 2 * pairs:2].set(donor - moved).at[2:2 + 2 * pairs:2].set(taker + moved)
    return tallies[jax.random.permutation(jax.random.fold_in(own_key, 2), count)]


def normal_values(rng, dims, scale, reach, split=(), kind=jnp.bfloat16):
    array = jax.random.normal(rng, dims, jnp.float32) * scale
    if len(split) > 0:
        array = levels(rng, dims, split, -0.22, 0.18) * array
    return jnp.clip(array, min=-reach, max=reach).astype(kind)


def setup_inputs(seed: int = 0) -> dict:
    seeds = jax.random.split(jax.random.key(seed), 6)
    return {
        "hidden": normal_values(seeds[0], (RELAY_SECTIONS, SEQUENCE_TOKENS, MODEL_WIDTH), 1.0, 6.0, ((0, 4), (1, 8))),
        "queries": draw_queries(jax.random.fold_in(seeds[5], 71), 0),
        "key_value_weight": normal_values(seeds[2], (RELAY_SECTIONS, MODEL_WIDTH, 2 * KEY_VALUE_HEADS * HEAD_SIZE), MODEL_WIDTH ** -0.5, 0.09375, ((0, 4),)),
        "doc_ids": jax.vmap(lambda own: jnp.searchsorted(jnp.cumsum(ragged(own, DOCS, SEQUENCE_TOKENS, SEQUENCE_TOKENS * 3 // 4, 2)), jnp.arange(SEQUENCE_TOKENS), side="right"))(jax.random.split(seeds[3], RELAY_SECTIONS)).reshape((RELAY_SECTIONS, SEQUENCE_TOKENS)).astype(jnp.int32),
        "scored": plant((jax.random.randint(seeds[4], (RELAY_SECTIONS, SEQUENCE_TOKENS), 0, 4) < 3).astype(jnp.int32), jax.random.fold_in(seeds[4], 1), 0, 1),
    }


rope_base = 500000.0

def apply_rotary(key_heads, token_positions):
    half_dim = key_heads.shape[-1] // 2
    frequency = rope_base ** (-jnp.arange(half_dim, dtype=jnp.float32) * 2.0 / key_heads.shape[-1])
    angles = token_positions.astype(jnp.float32)[:, None] * frequency[None, :]
    cosine_part = jnp.cos(angles)[:, None, :]
    sine_part = jnp.sin(angles)[:, None, :]
    lower_half = key_heads[..., :half_dim]
    upper_half = key_heads[..., half_dim:]
    return jnp.concatenate([lower_half * cosine_part - upper_half * sine_part, upper_half * cosine_part + lower_half * sine_part], axis=-1)

def one_phase(hidden_rows, query_rows, weight_rows, doc_rows, mask_rows):
    wide = hidden_rows.astype(jnp.float32)
    normed = (wide * lax.rsqrt(lax.optimization_barrier(jnp.mean(wide * wide, axis=-1, keepdims=True)) + 1e-05)).astype(jnp.bfloat16)
    projected_rows = jnp.dot(normed, weight_rows, preferred_element_type=jnp.float32)
    key_value_width = KEY_VALUE_HEADS * HEAD_SIZE
    token_positions = jnp.arange(SEQUENCE_TOKENS, dtype=jnp.int32)
    key_matrix = apply_rotary(projected_rows[:, :key_value_width].reshape(SEQUENCE_TOKENS, KEY_VALUE_HEADS, HEAD_SIZE), token_positions).astype(jnp.bfloat16)
    value_matrix = projected_rows[:, key_value_width:].reshape(SEQUENCE_TOKENS, KEY_VALUE_HEADS, HEAD_SIZE).astype(jnp.bfloat16)
    query_group_width = QUERY_HEADS // KEY_VALUE_HEADS
    key_wide = jnp.repeat(key_matrix.astype(jnp.float32), query_group_width, axis=1)
    value_wide = jnp.repeat(value_matrix.astype(jnp.float32), query_group_width, axis=1)
    block_len = math.gcd(SEQUENCE_TOKENS, 256)
    score_scale = 1.0 / math.sqrt(HEAD_SIZE)

    def attend(offset):
        query_block = lax.dynamic_slice_in_dim(query_rows, offset, block_len, 0).astype(jnp.float32).reshape(block_len, QUERY_HEADS, HEAD_SIZE)
        scores = jnp.einsum('qhd,khd->hqk', query_block, key_wide) * score_scale
        query_pos = offset + jnp.arange(block_len, dtype=jnp.int32)
        query_doc = lax.dynamic_slice_in_dim(doc_rows, offset, block_len, 0)
        allowed = (token_positions[None, :] <= query_pos[:, None]) & (doc_rows[None, :] == query_doc[:, None])
        scores = jnp.where(allowed[None], scores, jnp.float32(-1e+30))
        row_max = lax.optimization_barrier(jnp.max(scores, axis=-1, keepdims=True))
        expo = jnp.exp(scores - row_max)
        total = lax.optimization_barrier(jnp.sum(expo, axis=-1))
        weights = expo.astype(jnp.bfloat16)
        result = jnp.einsum('hqk,khd->hqd', weights.astype(jnp.float32), value_wide) / total[..., None]
        return jnp.transpose(result, (1, 0, 2)).reshape(block_len, QUERY_HEADS * HEAD_SIZE)
    starts = jnp.arange(SEQUENCE_TOKENS // block_len, dtype=jnp.int32) * block_len
    attended = lax.map(attend, starts).reshape(SEQUENCE_TOKENS, QUERY_HEADS * HEAD_SIZE)
    return (attended * mask_rows.astype(jnp.float32)[:, None]).astype(jnp.bfloat16)

def reference(hidden, queries, key_value_weight, doc_ids, scored):
    outputs = [one_phase(hidden[phase_idx], queries[phase_idx], key_value_weight[phase_idx], doc_ids[phase_idx], scored[phase_idx]) for phase_idx in range(RELAY_SECTIONS)]
    return jnp.roll(jnp.stack(outputs, axis=0), 1, axis=0)
```

```python
import functools
import math

import jax
import jax.numpy as jnp
import numpy as np
from jax import lax
from jax.experimental import pallas as pl
from jax.experimental.pallas import tpu as pltpu
from jax.sharding import PartitionSpec as P

QUERY_HEADS = 16
KEY_VALUE_HEADS = 4
HEAD_SIZE = 128
GROUP = QUERY_HEADS // KEY_VALUE_HEADS
GROUP_WIDTH = GROUP * HEAD_SIZE
PAIR_WIDTH = 2 * HEAD_SIZE
MASKED = -1e30

rope_base = 500000.0


def from_behind(block, axis, distance):
    devices = range(lax.axis_size(axis))
    route = [((i - distance) % len(devices), i) for i in devices]
    return lax.ppermute(block, axis, route)


def apply_rotary(key_heads, token_positions):
    half_dim = key_heads.shape[-1] // 2
    frequency = rope_base ** (-jnp.arange(half_dim, dtype=jnp.float32) * 2.0 / key_heads.shape[-1])
    angles = token_positions.astype(jnp.float32)[:, None] * frequency[None, :]
    cosine_part = jnp.cos(angles)[:, None, :]
    sine_part = jnp.sin(angles)[:, None, :]
    lower_half = key_heads[..., :half_dim]
    upper_half = key_heads[..., half_dim:]
    return jnp.concatenate(
        [
            lower_half * cosine_part - upper_half * sine_part,
            upper_half * cosine_part + lower_half * sine_part,
        ],
        axis=-1,
    )


def gathered_everywhere(hidden, queries, key_value_weight, doc_ids, scored):
    count_of_rows = hidden.shape[1]
    first_row = lax.axis_index("ctx") * count_of_rows
    token_positions = first_row + jnp.arange(count_of_rows, dtype=jnp.int32)
    wide = hidden[0].astype(jnp.float32)
    normed = (wide * lax.rsqrt(jnp.mean(wide * wide, axis=-1, keepdims=True) + 1e-05)).astype(
        jnp.bfloat16
    )
    projected_rows = jnp.dot(normed, key_value_weight[0], preferred_element_type=jnp.float32)
    key_value_width = KEY_VALUE_HEADS * HEAD_SIZE
    key_matrix = (
        apply_rotary(
            projected_rows[:, :key_value_width].reshape(count_of_rows, KEY_VALUE_HEADS, HEAD_SIZE),
            token_positions,
        )
        .astype(jnp.bfloat16)
        .reshape(count_of_rows, key_value_width)
    )
    value_matrix = projected_rows[:, key_value_width:].astype(jnp.bfloat16)
    query_head_count = queries[0].reshape(count_of_rows, KEY_VALUE_HEADS, GROUP, HEAD_SIZE)
    sequence_docs = doc_ids[0]
    own_docs = lax.dynamic_slice_in_dim(sequence_docs, first_row, count_of_rows, 0)
    score_scale = 1.0 / math.sqrt(HEAD_SIZE)
    stacked = jnp.concatenate([key_matrix, value_matrix], axis=1)
    collected_rows = lax.all_gather(stacked, "ctx", axis=0, tiled=True)
    sequence_length = collected_rows.shape[0]
    every_key_row = collected_rows[:, :key_value_width].reshape(
        sequence_length, KEY_VALUE_HEADS, HEAD_SIZE
    )
    every_value_row = collected_rows[:, key_value_width:].reshape(
        sequence_length, KEY_VALUE_HEADS, HEAD_SIZE
    )
    head_outputs = []
    for key_value_head in range(KEY_VALUE_HEADS):
        key_part = every_key_row[:, key_value_head : key_value_head + 1]
        key_count = key_part.shape[0]
        scores = (
            jnp.einsum(
                "qhgd,khd->hgqk",
                query_head_count[:, key_value_head : key_value_head + 1],
                key_part,
                preferred_element_type=jnp.float32,
            )
            * score_scale
        )
        key_pos = jnp.arange(key_count, dtype=jnp.int32)
        allowed = (key_pos[None, :] <= token_positions[:, None]) & (
            sequence_docs[None, :] == own_docs[:, None]
        )
        scores = jnp.where(allowed[None, None], scores, jnp.float32(MASKED))
        row_max = jnp.max(scores, axis=-1, keepdims=True)
        expo = jnp.exp(scores - row_max)
        total = jnp.sum(expo, axis=-1)
        weights = expo.astype(jnp.bfloat16)
        summed = jnp.einsum(
            "hgqk,khd->hgqd",
            weights,
            every_value_row[:, key_value_head : key_value_head + 1],
            preferred_element_type=jnp.float32,
        )
        head_outputs.append(summed / total[..., None])
    attended = jnp.transpose(jnp.concatenate(head_outputs, axis=0), (2, 0, 1, 3))
    flat = (
        attended.reshape(count_of_rows, QUERY_HEADS * HEAD_SIZE)
        * scored[0].astype(jnp.float32)[:, None]
    )
    outgoing = flat.astype(jnp.bfloat16)[None]
    return from_behind(outgoing, "phase", 1)


def rotary_table(positions):
    half = HEAD_SIZE // 2
    frequency = (rope_base ** (-np.arange(half) * 2.0 / HEAD_SIZE)).astype(np.float32)
    angles = (np.arange(positions, dtype=np.float32)[:, None] * frequency[None, :]).astype(np.float64)
    cosine, sine = np.cos(angles), np.sin(angles)
    return np.concatenate([cosine, cosine, -sine, sine], axis=1).astype(np.float32)


def project_kernel(
    blocks,
    hidden,
    table,
    queries,
    weight,
    keep_a,
    keep_b,
    give,
    q_a,
    q_a_give,
    q_b,
    q_b_give,
    weight_store,
    normed,
    weight_sems,
    query_sems,
):
    core = lax.rem(lax.axis_index("ctx"), 2)
    depth = weight.shape[1] // blocks
    copies = []
    for i in range(blocks):
        copy = pltpu.make_async_copy(
            weight.at[0, pl.ds(i * depth, depth), :], weight_store.at[i], weight_sems.at[i]
        )
        copy.start()
        copies.append(copy)
    first = core * (2 * GROUP_WIDTH)
    second = (1 - core) * (2 * GROUP_WIDTH)
    cuts = []
    for i, (start, target) in enumerate(
        (
            (first, q_a),
            (second, q_a_give),
            (first + GROUP_WIDTH, q_b),
            (second + GROUP_WIDTH, q_b_give),
        )
    ):
        cut = pltpu.make_async_copy(
            queries.at[0, :, pl.ds(pl.multiple_of(start, GROUP_WIDTH), GROUP_WIDTH)],
            target,
            query_sems.at[i],
        )
        cut.start()
        cuts.append(cut)
    wide = hidden[0].astype(jnp.float32)
    scale = lax.rsqrt(jnp.mean(wide * wide, axis=-1, keepdims=True) + 1e-05)
    normed[...] = (wide * scale).astype(jnp.bfloat16)
    total = None
    for i in range(blocks):
        copies[i].wait()
        part = jnp.dot(
            normed[:, i * depth : (i + 1) * depth],
            weight_store[i],
            preferred_element_type=jnp.float32,
        )
        total = part if total is None else total + part
    cosine, sine = table[:, :HEAD_SIZE], table[:, HEAD_SIZE:]
    pairs = []
    for head in range(KEY_VALUE_HEADS):
        key = total[:, head * HEAD_SIZE : (head + 1) * HEAD_SIZE]
        key = key * cosine + pltpu.roll(key, HEAD_SIZE // 2, 1) * sine
        at = (KEY_VALUE_HEADS + head) * HEAD_SIZE
        value = total[:, at : at + HEAD_SIZE]
        pairs.append(jnp.concatenate([key, value], axis=1).astype(jnp.bfloat16))

    for mine in range(2):

        @pl.when(core == mine)
        def _():
            keep_a[...] = pairs[2 * mine]
            keep_b[...] = pairs[2 * mine + 1]
            give[:, :PAIR_WIDTH] = pairs[2 * (1 - mine)]
            give[:, PAIR_WIDTH:] = pairs[2 * (1 - mine) + 1]

    for cut in cuts:
        cut.wait()


def project(hidden, queries, weight, table):
    rows, width = hidden.shape[1], hidden.shape[2]
    columns = weight.shape[2]
    blocks = 8
    pair = jax.ShapeDtypeStruct((rows, PAIR_WIDTH), jnp.bfloat16)
    cut = jax.ShapeDtypeStruct((rows, GROUP_WIDTH), jnp.bfloat16)
    vmem = pl.BlockSpec(memory_space=pltpu.VMEM)
    hbm = pl.BlockSpec(memory_space=pl.ANY)
    return pl.pallas_call(
        functools.partial(project_kernel, blocks),
        grid=(1,),
        out_shape=(
            pair,
            pair,
            jax.ShapeDtypeStruct((rows, 2 * PAIR_WIDTH), jnp.bfloat16),
            cut,
            cut,
            cut,
            cut,
        ),
        in_specs=[
            vmem,
            pl.BlockSpec((rows, 2 * HEAD_SIZE), lambda i: (lax.axis_index("ctx"), 0)),
            hbm,
            hbm,
        ],
        out_specs=(vmem, vmem, vmem, hbm, hbm, hbm, hbm),
        scratch_shapes=[
            pltpu.VMEM((blocks, width // blocks, columns), jnp.bfloat16),
            pltpu.VMEM((rows, width), jnp.bfloat16),
            pltpu.SemaphoreType.DMA((blocks,)),
            pltpu.SemaphoreType.DMA((4,)),
        ],
        compiler_params=pltpu.CompilerParams(vmem_limit_bytes=40 * 2**20),
        cost_estimate=pl.CostEstimate(
            flops=2 * rows * width * columns,
            bytes_accessed=2 * (width * columns + rows * width),
            transcendentals=0,
        ),
        name="project",
    )(hidden, table, queries, weight)


def attend_kernel(q_own, q_other, kv_0, kv_1, kv_2, kv_3, docs, out_own, out_other, bias):
    rows = q_own.shape[0]
    place = lax.axis_index("ctx")
    chip, core = place // 2, lax.rem(place, 2)
    cores = (core, 1 - core)
    row_at = lax.broadcasted_iota(jnp.int32, (rows, rows), 0)
    key_at = lax.broadcasted_iota(jnp.int32, (rows, rows), 1)

    def docs_of(device):
        start = pl.multiple_of(device * rows, rows)
        row = docs[:, pl.ds(start, rows)].astype(jnp.float32)
        return jnp.broadcast_to(row, (rows, rows))

    for a in range(2):
        query_docs = docs_of(2 * chip + cores[a]).T
        for back in range(4):
            for b in range(2):
                block = chip - back
                key_docs = docs_of(2 * jnp.maximum(block, 0) + cores[b])
                key_docs = jnp.where(block >= 0, key_docs, -1.0)
                allowed = query_docs == key_docs
                if back == 0:
                    allowed &= cores[a] * rows + row_at >= cores[b] * rows + key_at
                at = (2 * back + b) * rows
                bias[a * rows : (a + 1) * rows, at : at + rows] = jnp.where(allowed, 0.0, MASKED)

    blocks = (kv_0, kv_1, kv_2, kv_3)
    factor = math.log2(math.e) / math.sqrt(HEAD_SIZE)
    for head in range(GROUP):
        at = head * HEAD_SIZE
        q = jnp.concatenate([q_own[:, at : at + HEAD_SIZE], q_other[:, at : at + HEAD_SIZE]], axis=0)
        scores = []
        for back, kv in enumerate(blocks):
            part = lax.dot_general(
                q,
                kv[:, :HEAD_SIZE],
                (((1,), (1,)), ((), ())),
                preferred_element_type=jnp.float32,
            )
            scores.append(part + bias[:, 2 * back * rows : 2 * (back + 1) * rows])
        scores = jnp.concatenate(scores, axis=1)
        row_max = jnp.max(scores, axis=-1, keepdims=True)
        expo = jnp.exp2((scores - row_max) * factor)
        total = jnp.sum(expo, axis=-1, keepdims=True)
        weights = expo.astype(jnp.bfloat16)
        summed = None
        for back, kv in enumerate(blocks):
            part = jnp.dot(
                weights[:, 2 * back * rows : 2 * (back + 1) * rows],
                kv[:, HEAD_SIZE:],
                preferred_element_type=jnp.float32,
            )
            summed = part if summed is None else summed + part
        result = (summed / total).astype(jnp.bfloat16)
        out_own[:, at : at + HEAD_SIZE] = result[:rows]
        out_other[:, at : at + HEAD_SIZE] = result[rows:]


def attend(q_own, q_other, blocks, docs):
    rows = q_own.shape[0]
    vmem = pl.BlockSpec(memory_space=pltpu.VMEM)
    out = jax.ShapeDtypeStruct((rows, GROUP_WIDTH), jnp.bfloat16)
    work = GROUP * 2 * rows * 8 * rows
    return pl.pallas_call(
        attend_kernel,
        out_shape=(out, out),
        in_specs=[vmem] * 7,
        out_specs=(vmem, vmem),
        scratch_shapes=[pltpu.VMEM((2 * rows, 8 * rows), jnp.float32)],
        compiler_params=pltpu.CompilerParams(vmem_limit_bytes=40 * 2**20),
        cost_estimate=pl.CostEstimate(
            flops=4 * work * HEAD_SIZE, bytes_accessed=2**20, transcendentals=work
        ),
        name="attend",
    )(q_own, q_other, *blocks, docs)


def assemble_kernel(a_own, a_other, b_own, b_other, notes, out):
    rows = a_own.shape[0]
    core = lax.rem(lax.axis_index("ctx"), 2)
    kept = notes[:, notes.shape[1] - rows :].astype(jnp.float32)
    kept = jnp.broadcast_to(kept, (rows, rows)).T

    def put(at, part):
        for i in range(GROUP):
            cut = part[:, i * HEAD_SIZE : (i + 1) * HEAD_SIZE].astype(jnp.float32) * kept
            out[0, :, at + i * HEAD_SIZE : at + (i + 1) * HEAD_SIZE] = cut.astype(jnp.bfloat16)

    for mine in range(2):

        @pl.when(core == mine)
        def _():
            put(2 * mine * GROUP_WIDTH, a_own)
            put((2 * mine + 1) * GROUP_WIDTH, b_own)
            put(2 * (1 - mine) * GROUP_WIDTH, a_other)
            put((2 * (1 - mine) + 1) * GROUP_WIDTH, b_other)


def assemble(a_own, a_other, b_own, b_other, notes):
    rows = a_own.shape[0]
    vmem = pl.BlockSpec(memory_space=pltpu.VMEM)
    return pl.pallas_call(
        assemble_kernel,
        out_shape=jax.ShapeDtypeStruct((1, rows, QUERY_HEADS * HEAD_SIZE), jnp.bfloat16),
        in_specs=[vmem] * 5,
        out_specs=vmem,
        name="assemble",
    )(a_own, a_other, b_own, b_other, notes)


def up(block, chips, first=0):
    count = lax.axis_size("ctx")
    route = [(i, i + 2 * chips) for i in range(2 * first, count - 2 * chips)]
    return lax.ppermute(block, "ctx", route)


def across(block):
    return lax.ppermute(block, "ctx", [(i, i ^ 1) for i in range(lax.axis_size("ctx"))])


def onward(block, cross=0):
    sections, count = lax.axis_size("phase"), lax.axis_size("ctx")
    route = [
        (p * count + c, (p + 1) % sections * count + (c ^ cross))
        for p in range(sections)
        for c in range(count)
    ]
    return lax.ppermute(block, ("phase", "ctx"), route)


def behind(block):
    one = up(block, 1)
    two = up(one, 1, 1)
    three = up(one, 2, 1)
    return one, two, three


def relayed(hidden, queries, key_value_weight, doc_ids, scored):
    table = jnp.asarray(rotary_table(doc_ids.shape[1]))
    notes = onward(jnp.concatenate([doc_ids, scored], axis=1))
    keep_a, keep_b, give, q_a, q_a_give, q_b, q_b_give = project(
        hidden, queries, key_value_weight, table
    )
    taken = across(give)
    block_a = jnp.concatenate([keep_a, taken[:, :PAIR_WIDTH]], axis=0)
    block_b = jnp.concatenate([keep_b, taken[:, PAIR_WIDTH:]], axis=0)
    far_a = behind(block_a)
    block_b = onward(block_b)
    q_a_other = across(q_a_give)
    q_b_own = onward(q_b)
    q_b_other = onward(q_b_give, 1)
    far_b = behind(block_b)
    a_own, a_other = attend(q_a, q_a_other, (block_a,) + far_a, doc_ids)
    a_own = onward(a_own)
    a_other = onward(a_other, 1)
    b_own, b_other = attend(q_b_own, q_b_other, (block_b,) + far_b, notes)
    b_other = across(b_other)
    return assemble(a_own, a_other, b_own, b_other, notes)


def solution(mesh):
    placed = (
        P("phase", "ctx", None),
        P("phase", "ctx", None),
        P("phase", None, None),
        P("phase", None),
        P("phase", "ctx"),
    )
    plan = relayed if mesh.shape["ctx"] == 8 else gathered_everywhere
    return jax.shard_map(
        plan, mesh=mesh, in_specs=placed, out_specs=P("phase", "ctx", None), check_vma=False
    )
```

```python
import functools
import math

import jax
import jax.numpy as jnp
import numpy as np
from jax import lax
from jax.experimental import pallas as pl
from jax.experimental.pallas import tpu as pltpu
from jax.sharding import PartitionSpec as P

QUERY_HEADS = 16
KEY_VALUE_HEADS = 4
HEAD_SIZE = 128
GROUP = QUERY_HEADS // KEY_VALUE_HEADS
GROUP_WIDTH = GROUP * HEAD_SIZE
PAIR_WIDTH = 2 * HEAD_SIZE
MASKED = -1e30
NOTE_ROWS = 16

rope_base = 500000.0


def from_behind(block, axis, distance):
    devices = range(lax.axis_size(axis))
    route = [((i - distance) % len(devices), i) for i in devices]
    return lax.ppermute(block, axis, route)


def apply_rotary(key_heads, token_positions):
    half_dim = key_heads.shape[-1] // 2
    frequency = rope_base ** (-jnp.arange(half_dim, dtype=jnp.float32) * 2.0 / key_heads.shape[-1])
    angles = token_positions.astype(jnp.float32)[:, None] * frequency[None, :]
    cosine_part = jnp.cos(angles)[:, None, :]
    sine_part = jnp.sin(angles)[:, None, :]
    lower_half = key_heads[..., :half_dim]
    upper_half = key_heads[..., half_dim:]
    return jnp.concatenate(
        [
            lower_half * cosine_part - upper_half * sine_part,
            upper_half * cosine_part + lower_half * sine_part,
        ],
        axis=-1,
    )


def gathered_everywhere(hidden, queries, key_value_weight, doc_ids, scored):
    count_of_rows = hidden.shape[1]
    first_row = lax.axis_index("ctx") * count_of_rows
    token_positions = first_row + jnp.arange(count_of_rows, dtype=jnp.int32)
    wide = hidden[0].astype(jnp.float32)
    normed = (wide * lax.rsqrt(jnp.mean(wide * wide, axis=-1, keepdims=True) + 1e-05)).astype(
        jnp.bfloat16
    )
    projected_rows = jnp.dot(normed, key_value_weight[0], preferred_element_type=jnp.float32)
    key_value_width = KEY_VALUE_HEADS * HEAD_SIZE
    key_matrix = (
        apply_rotary(
            projected_rows[:, :key_value_width].reshape(count_of_rows, KEY_VALUE_HEADS, HEAD_SIZE),
            token_positions,
        )
        .astype(jnp.bfloat16)
        .reshape(count_of_rows, key_value_width)
    )
    value_matrix = projected_rows[:, key_value_width:].astype(jnp.bfloat16)
    query_head_count = queries[0].reshape(count_of_rows, KEY_VALUE_HEADS, GROUP, HEAD_SIZE)
    sequence_docs = doc_ids[0]
    own_docs = lax.dynamic_slice_in_dim(sequence_docs, first_row, count_of_rows, 0)
    score_scale = 1.0 / math.sqrt(HEAD_SIZE)
    stacked = jnp.concatenate([key_matrix, value_matrix], axis=1)
    collected_rows = lax.all_gather(stacked, "ctx", axis=0, tiled=True)
    sequence_length = collected_rows.shape[0]
    every_key_row = collected_rows[:, :key_value_width].reshape(
        sequence_length, KEY_VALUE_HEADS, HEAD_SIZE
    )
    every_value_row = collected_rows[:, key_value_width:].reshape(
        sequence_length, KEY_VALUE_HEADS, HEAD_SIZE
    )
    head_outputs = []
    for key_value_head in range(KEY_VALUE_HEADS):
        key_part = every_key_row[:, key_value_head : key_value_head + 1]
        key_count = key_part.shape[0]
        scores = (
            jnp.einsum(
                "qhgd,khd->hgqk",
                query_head_count[:, key_value_head : key_value_head + 1],
                key_part,
                preferred_element_type=jnp.float32,
            )
            * score_scale
        )
        key_pos = jnp.arange(key_count, dtype=jnp.int32)
        allowed = (key_pos[None, :] <= token_positions[:, None]) & (
            sequence_docs[None, :] == own_docs[:, None]
        )
        scores = jnp.where(allowed[None, None], scores, jnp.float32(MASKED))
        row_max = jnp.max(scores, axis=-1, keepdims=True)
        expo = jnp.exp(scores - row_max)
        total = jnp.sum(expo, axis=-1)
        weights = expo.astype(jnp.bfloat16)
        summed = jnp.einsum(
            "hgqk,khd->hgqd",
            weights,
            every_value_row[:, key_value_head : key_value_head + 1],
            preferred_element_type=jnp.float32,
        )
        head_outputs.append(summed / total[..., None])
    attended = jnp.transpose(jnp.concatenate(head_outputs, axis=0), (2, 0, 1, 3))
    flat = (
        attended.reshape(count_of_rows, QUERY_HEADS * HEAD_SIZE)
        * scored[0].astype(jnp.float32)[:, None]
    )
    outgoing = flat.astype(jnp.bfloat16)[None]
    return from_behind(outgoing, "phase", 1)


def rotary_tables(rows, devices):
    half = HEAD_SIZE // 2
    frequency = (rope_base ** (-np.arange(half) * 2.0 / HEAD_SIZE)).astype(np.float32).astype(np.float64)
    frequency = np.concatenate([frequency, frequency])[None, :]
    within = np.arange(rows)[:, None] * frequency
    starts = np.arange(devices)[:, None] * (rows * frequency)
    return [
        jnp.asarray(np.concatenate([np.cos(x), np.sin(x)], axis=1), jnp.float32)
        for x in (within, starts)
    ]


def parity():
    return lax.rem(lax.axis_index("ctx") // 2, 2)


def project_kernel(
    cuts,
    hidden,
    weight,
    queries,
    within,
    starts,
    docs,
    scored,
    mine,
    other,
    swap,
    away,
    packed,
    wide,
    store,
    normed,
    hidden_sem,
    query_sems,
    weight_sems,
):
    rows, width = wide.shape[0], packed.shape[1]
    odd = parity()
    load_hidden = pltpu.make_async_copy(hidden.at[0], wide, hidden_sem)
    load_hidden.start()
    copies = []
    for i, (start, stop) in enumerate(cuts):
        span = pl.ds(start, stop - start)
        copy = pltpu.make_async_copy(weight.at[0, span, :], store.at[span, :], weight_sems.at[i])
        copy.start()
        copies.append(copy)
    asked = pl.ds(pl.multiple_of((1 - odd) * GROUP_WIDTH, GROUP_WIDTH), GROUP_WIDTH)
    cut_queries = [
        pltpu.make_async_copy(
            queries.at[0, :, asked], swap.at[pl.ds(0, rows), pl.ds(PAIR_WIDTH, GROUP_WIDTH)], query_sems.at[0]
        ),
        pltpu.make_async_copy(
            queries.at[0, :, pl.ds(width, width)], packed.at[pl.ds(0, rows), :], query_sems.at[1]
        ),
    ]
    for copy in cut_queries:
        copy.start()
    marks = jnp.concatenate([scored[...]] * (width // rows), axis=1)
    notes = [docs[...], marks, jnp.zeros((NOTE_ROWS - 2, width), jnp.int32)]
    notes = jnp.concatenate(notes, axis=0).astype(jnp.float32).astype(jnp.bfloat16)
    packed[rows:, :] = notes
    swap[rows:, :] = notes[:, : swap.shape[1]]
    base = starts[pl.ds(lax.axis_index("ctx"), 1), :]
    base_cosine, base_sine = base[:, :HEAD_SIZE], base[:, HEAD_SIZE:]
    cosine, sine = within[:, :HEAD_SIZE], within[:, HEAD_SIZE:]
    cosine, sine = (
        cosine * base_cosine - sine * base_sine,
        sine * base_cosine + cosine * base_sine,
    )
    sine = jnp.where(lax.broadcasted_iota(jnp.int32, sine.shape, 1) < HEAD_SIZE // 2, -sine, sine)
    load_hidden.wait()
    values = wide[...].astype(jnp.float32)
    scale = lax.rsqrt(jnp.mean(values * values, axis=-1, keepdims=True) + 1e-05)
    normed[...] = (values * scale).astype(jnp.bfloat16)
    total = None
    for copy, (start, stop) in zip(copies, cuts):
        copy.wait()
        part = jnp.dot(
            normed[:, start:stop], store[start:stop, :], preferred_element_type=jnp.float32
        )
        total = part if total is None else total + part
    pairs = []
    for head in range(KEY_VALUE_HEADS):
        key = total[:, head * HEAD_SIZE : (head + 1) * HEAD_SIZE]
        key = key * cosine + pltpu.roll(key, HEAD_SIZE // 2, 1) * sine
        at = (KEY_VALUE_HEADS + head) * HEAD_SIZE
        value = total[:, at : at + HEAD_SIZE]
        pairs.append(jnp.concatenate([key, value], axis=1).astype(jnp.bfloat16))
    away[:, :PAIR_WIDTH] = pairs[2]
    away[:, PAIR_WIDTH:] = pairs[3]
    for u in range(2):

        @pl.when(odd == u)
        def _():
            mine[...] = pairs[u]
            other[...] = pairs[1 - u]
            swap[:rows, :PAIR_WIDTH] = pairs[1 - u]

    for copy in cut_queries:
        copy.wait()


def project(hidden, weight, queries, docs, scored):
    rows, width = hidden.shape[1], hidden.shape[2]
    columns = weight.shape[2]
    cuts = ((0, width // 2), (width // 2, width))
    within, starts = rotary_tables(rows, docs.shape[1] // rows)
    hbm = pl.BlockSpec(memory_space=pltpu.HBM)
    vmem = pl.BlockSpec(memory_space=pltpu.VMEM)
    pair = jax.ShapeDtypeStruct((rows, PAIR_WIDTH), jnp.bfloat16)
    return pl.pallas_call(
        functools.partial(project_kernel, cuts),
        out_shape=(
            pair,
            pair,
            jax.ShapeDtypeStruct((rows + NOTE_ROWS, PAIR_WIDTH + GROUP_WIDTH), jnp.bfloat16),
            jax.ShapeDtypeStruct((rows, 2 * PAIR_WIDTH), jnp.bfloat16),
            jax.ShapeDtypeStruct((rows + NOTE_ROWS, 2 * GROUP_WIDTH), jnp.bfloat16),
        ),
        in_specs=[hbm, hbm, hbm, vmem, vmem, vmem, vmem],
        out_specs=(vmem,) * 5,
        scratch_shapes=[
            pltpu.VMEM((rows, width), jnp.bfloat16),
            pltpu.VMEM((width, columns), jnp.bfloat16),
            pltpu.VMEM((rows, width), jnp.bfloat16),
            pltpu.SemaphoreType.DMA,
            pltpu.SemaphoreType.DMA((2,)),
            pltpu.SemaphoreType.DMA((len(cuts),)),
        ],
        compiler_params=pltpu.CompilerParams(vmem_limit_bytes=63 * 2**20),
        cost_estimate=pl.CostEstimate(flops=0, bytes_accessed=0, transcendentals=0),
        name="project",
    )(hidden, weight, queries, within, starts, docs, scored)


def attend_body(q, kvs, doc_row, kept, bias, put):
    rows = q.shape[0]
    place = lax.axis_index("ctx")
    chip, core = place // 2, lax.rem(place, 2)
    cores = (core, 1 - core)

    def docs_of(device):
        row = doc_row(pl.ds(pl.multiple_of(device * rows, rows), rows))
        return jnp.broadcast_to(row.astype(jnp.float32), (rows, rows))

    query_docs = docs_of(place).T
    for back in range(4):
        for b in range(2):
            block = chip - back
            key_docs = docs_of(2 * jnp.maximum(block, 0) + cores[b])
            allowed = query_docs == jnp.where(block >= 0, key_docs, -1.0)
            if back == 0:
                row_at = lax.broadcasted_iota(jnp.int32, (rows, rows), 0)
                key_at = lax.broadcasted_iota(jnp.int32, (rows, rows), 1)
                allowed &= core * rows + row_at >= cores[b] * rows + key_at
            at = (2 * back + b) * rows
            bias[:, at : at + rows] = jnp.where(allowed, 0.0, MASKED)

    kept_rows = jnp.broadcast_to(kept, (rows, rows)).T[:, :1]
    factor = math.log2(math.e) / math.sqrt(HEAD_SIZE)
    for head in range(2):
        at = head * PAIR_WIDTH
        for half in range(GROUP // 2):
            first = (head * GROUP + 2 * half) * HEAD_SIZE
            pair = jnp.concatenate(
                [q[:, first : first + HEAD_SIZE], q[:, first + HEAD_SIZE : first + 2 * HEAD_SIZE]],
                axis=0,
            )
            scores = []
            for back in range(4):
                keys = jnp.concatenate(
                    [kvs[2 * back + b][:, at : at + HEAD_SIZE] for b in range(2)], axis=0
                )
                part = lax.dot_general(
                    pair, keys, (((1,), (1,)), ((), ())), preferred_element_type=jnp.float32
                )
                block_bias = bias[:, 2 * back * rows : 2 * (back + 1) * rows]
                scores.append(part + jnp.concatenate([block_bias, block_bias], axis=0))
            scores = jnp.concatenate(scores, axis=1)
            row_max = jnp.max(scores, axis=-1, keepdims=True)
            expo = jnp.exp2((scores - row_max) * factor)
            total = jnp.sum(expo, axis=-1, keepdims=True)
            weights = expo.astype(jnp.bfloat16)
            summed = None
            for back in range(4):
                values = jnp.concatenate(
                    [
                        kvs[2 * back + b][:, at + HEAD_SIZE : at + 2 * HEAD_SIZE]
                        for b in range(2)
                    ],
                    axis=0,
                )
                part = jnp.dot(
                    weights[:, 2 * back * rows : 2 * (back + 1) * rows],
                    values,
                    preferred_element_type=jnp.float32,
                )
                summed = part if summed is None else summed + part
            result = summed / total
            for i in range(2):
                put(
                    first + i * HEAD_SIZE,
                    (result[i * rows : (i + 1) * rows] * kept_rows).astype(jnp.bfloat16),
                )


def attend_home_kernel(
    queries, swap, mine, mine_x, near_x, far, far_x, beyond, beyond_x, docs, scored, out_own, out_other, bias
):
    rows = queries.shape[1]
    place = lax.axis_index("ctx")
    chip, core = place // 2, lax.rem(place, 2)
    partner = place + 2 - 4 * lax.rem(chip, 2)
    behind = place - 4
    crossed = 2 * (3 - chip) + core
    far_off = chip >= 2

    def other_core(device):
        return device + 1 - 2 * lax.rem(device, 2)

    def docs_of(device):
        start = pl.multiple_of(device * rows, rows)
        return jnp.broadcast_to(docs[:, pl.ds(start, rows)].astype(jnp.float32), (rows, rows))

    row_at = lax.broadcasted_iota(jnp.int32, (rows, rows), 0)
    key_at = lax.broadcasted_iota(jnp.int32, (rows, rows), 1)
    sources = []
    for device in (place, partner, behind, crossed):
        device = jnp.where(far_off, device, lax.rem(device + 8, 8))
        sources += [device, other_core(device)]
    query_docs = [docs_of(place).T, docs_of(partner).T]
    for k, device in enumerate(sources):
        key_docs = docs_of(device)
        if k >= 4:
            key_docs = jnp.where(far_off, key_docs, -1.0)
        for a, asker in enumerate((place, partner)):
            allowed = query_docs[a] == key_docs
            if k < 4:
                allowed &= asker * rows + row_at >= device * rows + key_at
            bias[a * rows : (a + 1) * rows, k * rows : (k + 1) * rows] = jnp.where(
                allowed, 0.0, MASKED
            )

    def blocks(at):
        cut = slice(at, at + HEAD_SIZE)
        return [
            jnp.concatenate([one[:rows, cut], twin[:, cut]], axis=0)
            for one, twin in ((mine, mine_x), (swap, near_x), (far, far_x), (beyond, beyond_x))
        ]

    kept = jnp.concatenate(
        [
            jnp.broadcast_to(row, (rows, rows)).T[:, :1]
            for row in (
                scored[...].astype(jnp.float32),
                swap[rows:, :rows].astype(jnp.float32)[1:2],
            )
        ],
        axis=0,
    )
    keys, values = blocks(0), blocks(HEAD_SIZE)
    factor = math.log2(math.e) / math.sqrt(HEAD_SIZE)
    for head in range(GROUP):
        at = head * HEAD_SIZE
        q = jnp.concatenate(
            [queries[0, :, at : at + HEAD_SIZE], swap[:rows, PAIR_WIDTH + at : PAIR_WIDTH + at + HEAD_SIZE]], axis=0
        )
        scores = jnp.concatenate(
            [
                lax.dot_general(q, k, (((1,), (1,)), ((), ())), preferred_element_type=jnp.float32)
                for k in keys
            ],
            axis=1,
        )
        scores = scores + bias[...]
        row_max = jnp.max(scores, axis=-1, keepdims=True)
        expo = jnp.exp2((scores - row_max) * factor)
        total = jnp.sum(expo, axis=-1, keepdims=True)
        weights = expo.astype(jnp.bfloat16)
        summed = None
        for i, value in enumerate(values):
            part = jnp.dot(
                weights[:, 2 * i * rows : 2 * (i + 1) * rows],
                value,
                preferred_element_type=jnp.float32,
            )
            summed = part if summed is None else summed + part
        result = (summed / total * kept).astype(jnp.bfloat16)
        out_own[:, at : at + HEAD_SIZE] = result[:rows]
        out_other[:, at : at + HEAD_SIZE] = result[rows:]


class Halves:
    def __init__(self, first, second):
        self.refs = (first, second)
        self.width = first.shape[1]

    def __getitem__(self, index):
        rows, columns = index
        start = columns.start % self.width
        ref = self.refs[columns.start // self.width]
        return ref[rows, start : start + columns.stop - columns.start]


def attend_relayed_kernel(packed, *refs):
    kvs, (out, bias) = refs[:10], refs[10:]
    kvs = kvs[:5] + (Halves(*kvs[5:7]), kvs[7], Halves(*kvs[8:]))
    rows = out.shape[0]
    kept = packed[rows : rows + NOTE_ROWS, :rows].astype(jnp.float32)[1:2]

    def doc_row(at):
        return packed[rows : rows + NOTE_ROWS, at].astype(jnp.float32)[:1]

    def put(at, value):
        out[:, at : at + HEAD_SIZE] = value

    attend_body(packed.at[pl.ds(0, rows), :], kvs, doc_row, kept, bias, put)


def attend_cost(rows, flops):
    return dict(
        scratch_shapes=[pltpu.VMEM((rows, 8 * rows), jnp.float32)],
        compiler_params=pltpu.CompilerParams(vmem_limit_bytes=32 * 2**20),
        cost_estimate=pl.CostEstimate(flops=flops, bytes_accessed=0, transcendentals=0),
    )


def attend_home(queries, *rest):
    rows = queries.shape[1]
    out = jax.ShapeDtypeStruct((rows, GROUP_WIDTH), jnp.bfloat16)

    def whole(array):
        return pl.BlockSpec(array.shape, lambda i: (0,) * array.ndim)

    cost = attend_cost(rows, HOME_FLOPS)
    cost["scratch_shapes"] = [pltpu.VMEM((2 * rows, 8 * rows), jnp.float32)]
    return pl.pallas_call(
        attend_home_kernel,
        grid=(1,),
        out_shape=(out, out),
        in_specs=[pl.BlockSpec((1, rows, GROUP_WIDTH), lambda i: (0, 0, parity()))]
        + [whole(x) for x in rest],
        out_specs=(pl.BlockSpec((rows, GROUP_WIDTH), lambda i: (0, 0)),) * 2,
        name="attend_home",
        **cost,
    )(queries, *rest)


def attend_relayed(packed, kvs):
    rows, width = kvs[0].shape[0], packed.shape[1]
    vmem = pl.BlockSpec(memory_space=pltpu.VMEM)
    return pl.pallas_call(
        attend_relayed_kernel,
        out_shape=jax.ShapeDtypeStruct((rows, width), jnp.bfloat16),
        in_specs=[vmem] * 11,
        out_specs=vmem,
        name="attend_relayed",
        **attend_cost(rows, RELAYED_FLOPS),
    )(packed, *kvs)


def send(block, route):
    pairs = [(2 * a + core, 2 * b + core) for a, b in route for core in range(2)]
    return lax.ppermute(block, "ctx", pairs)


def across(block):
    return lax.ppermute(block, "ctx", [(i, i ^ 1) for i in range(lax.axis_size("ctx"))])


def onward(block, change=0):
    sections, count = lax.axis_size("phase"), lax.axis_size("ctx")
    route = [
        (p * count + c, (p + 1) % sections * count + (c ^ change))
        for p in range(sections)
        for c in range(count)
    ]
    return lax.ppermute(block, ("phase", "ctx"), route)


HOME_FLOPS = 2 * 10**9
RELAYED_FLOPS = 0


def after(block, *others):
    return lax.optimization_barrier((block,) + others)[0]


def across_halves(block):
    half = block.shape[1] // 2
    return across(block[:, :half]), across(block[:, half:])


def paired(hidden, queries, key_value_weight, doc_ids, scored):
    mine, other, swap, away, packed = project(hidden, key_value_weight, queries, doc_ids, scored)
    away = onward(away)
    swap = send(swap, ((0, 1), (1, 0), (2, 3), (3, 2)))
    far = send(mine, ((0, 2), (1, 3)))
    beyond = send(other, ((0, 3), (1, 2)))
    packed = onward(after(packed, swap))
    away_1 = send(away, ((0, 1), (1, 2), (2, 3)))
    away_2 = send(away_1, ((1, 2), (2, 3)))
    away_3 = send(away_1, ((1, 3),))
    swap, far, beyond = lax.optimization_barrier((swap, far, beyond))
    own, partners = attend_home(
        queries,
        swap,
        mine,
        across(mine),
        across(swap[: mine.shape[0], :PAIR_WIDTH]),
        far,
        across(far),
        beyond,
        across(beyond),
        doc_ids,
        scored,
    )
    own, partners = onward(own), onward(partners, 2)
    away = [away, across(away), away_1, across(after(away_1, packed))] + [
        x for block in (away_2, away_3) for x in (block, *across_halves(block))
    ]
    last = attend_relayed(packed, away)
    straight = jnp.concatenate([own, partners, last], axis=1)
    crossed = jnp.concatenate([partners, own, last], axis=1)
    return jnp.where(parity() == 1, crossed, straight)[None]


def solution(mesh):
    placed = (
        P("phase", "ctx", None),
        P("phase", "ctx", None),
        P("phase", None, None),
        P("phase", None),
        P("phase", "ctx"),
    )
    plan = paired if mesh.shape["ctx"] == 8 else gathered_everywhere
    return jax.shard_map(
        plan, mesh=mesh, in_specs=placed, out_specs=P("phase", "ctx", None), check_vma=False
    )
```

```python
import functools
import math

import jax
import jax.numpy as jnp
import numpy as np
from jax import lax
from jax.experimental import pallas as pl
from jax.experimental.pallas import tpu as pltpu
from jax.sharding import PartitionSpec as P

QUERY_HEADS = 16
KEY_VALUE_HEADS = 4
HEAD_SIZE = 128
GROUP = QUERY_HEADS // KEY_VALUE_HEADS
GROUP_WIDTH = GROUP * HEAD_SIZE
PAIR_WIDTH = 2 * HEAD_SIZE
MASKED = -1e30
NOTE_ROWS = 16

rope_base = 500000.0


def from_behind(block, axis, distance):
    devices = range(lax.axis_size(axis))
    route = [((i - distance) % len(devices), i) for i in devices]
    return lax.ppermute(block, axis, route)


def apply_rotary(key_heads, token_positions):
    half_dim = key_heads.shape[-1] // 2
    frequency = rope_base ** (-jnp.arange(half_dim, dtype=jnp.float32) * 2.0 / key_heads.shape[-1])
    angles = token_positions.astype(jnp.float32)[:, None] * frequency[None, :]
    cosine_part = jnp.cos(angles)[:, None, :]
    sine_part = jnp.sin(angles)[:, None, :]
    lower_half = key_heads[..., :half_dim]
    upper_half = key_heads[..., half_dim:]
    return jnp.concatenate(
        [
            lower_half * cosine_part - upper_half * sine_part,
            upper_half * cosine_part + lower_half * sine_part,
        ],
        axis=-1,
    )


def gathered_everywhere(hidden, queries, key_value_weight, doc_ids, scored):
    count_of_rows = hidden.shape[1]
    first_row = lax.axis_index("ctx") * count_of_rows
    token_positions = first_row + jnp.arange(count_of_rows, dtype=jnp.int32)
    wide = hidden[0].astype(jnp.float32)
    normed = (wide * lax.rsqrt(jnp.mean(wide * wide, axis=-1, keepdims=True) + 1e-05)).astype(
        jnp.bfloat16
    )
    projected_rows = jnp.dot(normed, key_value_weight[0], preferred_element_type=jnp.float32)
    key_value_width = KEY_VALUE_HEADS * HEAD_SIZE
    key_matrix = (
        apply_rotary(
            projected_rows[:, :key_value_width].reshape(count_of_rows, KEY_VALUE_HEADS, HEAD_SIZE),
            token_positions,
        )
        .astype(jnp.bfloat16)
        .reshape(count_of_rows, key_value_width)
    )
    value_matrix = projected_rows[:, key_value_width:].astype(jnp.bfloat16)
    query_head_count = queries[0].reshape(count_of_rows, KEY_VALUE_HEADS, GROUP, HEAD_SIZE)
    sequence_docs = doc_ids[0]
    own_docs = lax.dynamic_slice_in_dim(sequence_docs, first_row, count_of_rows, 0)
    score_scale = 1.0 / math.sqrt(HEAD_SIZE)
    stacked = jnp.concatenate([key_matrix, value_matrix], axis=1)
    collected_rows = lax.all_gather(stacked, "ctx", axis=0, tiled=True)
    sequence_length = collected_rows.shape[0]
    every_key_row = collected_rows[:, :key_value_width].reshape(
        sequence_length, KEY_VALUE_HEADS, HEAD_SIZE
    )
    every_value_row = collected_rows[:, key_value_width:].reshape(
        sequence_length, KEY_VALUE_HEADS, HEAD_SIZE
    )
    head_outputs = []
    for key_value_head in range(KEY_VALUE_HEADS):
        key_part = every_key_row[:, key_value_head : key_value_head + 1]
        key_count = key_part.shape[0]
        scores = (
            jnp.einsum(
                "qhgd,khd->hgqk",
                query_head_count[:, key_value_head : key_value_head + 1],
                key_part,
                preferred_element_type=jnp.float32,
            )
            * score_scale
        )
        key_pos = jnp.arange(key_count, dtype=jnp.int32)
        allowed = (key_pos[None, :] <= token_positions[:, None]) & (
            sequence_docs[None, :] == own_docs[:, None]
        )
        scores = jnp.where(allowed[None, None], scores, jnp.float32(MASKED))
        row_max = jnp.max(scores, axis=-1, keepdims=True)
        expo = jnp.exp(scores - row_max)
        total = jnp.sum(expo, axis=-1)
        weights = expo.astype(jnp.bfloat16)
        summed = jnp.einsum(
            "hgqk,khd->hgqd",
            weights,
            every_value_row[:, key_value_head : key_value_head + 1],
            preferred_element_type=jnp.float32,
        )
        head_outputs.append(summed / total[..., None])
    attended = jnp.transpose(jnp.concatenate(head_outputs, axis=0), (2, 0, 1, 3))
    flat = (
        attended.reshape(count_of_rows, QUERY_HEADS * HEAD_SIZE)
        * scored[0].astype(jnp.float32)[:, None]
    )
    outgoing = flat.astype(jnp.bfloat16)[None]
    return from_behind(outgoing, "phase", 1)


def rotary_table(rows, devices):
    half = HEAD_SIZE // 2
    frequency = (rope_base ** (-np.arange(half) * 2.0 / HEAD_SIZE)).astype(np.float32).astype(np.float64)
    frequency = np.concatenate([frequency, frequency])[None, :]
    angles = np.concatenate([np.arange(rows), rows * np.arange(devices)])[:, None] * frequency
    return jnp.asarray(np.concatenate([np.cos(angles), np.sin(angles)], axis=1), jnp.float32)


def parity():
    return lax.rem(lax.axis_index("ctx") // 2, 2)


def project_kernel(
    cuts,
    hidden,
    weight,
    queries,
    table,
    docs,
    scored,
    mine,
    other,
    swap,
    away,
    packed,
    wide,
    store,
    normed,
    angles,
    doc_row,
    scored_row,
    mine_out,
    other_out,
    swap_out,
    away_out,
    packed_out,
    in_sems,
    weight_sems,
    out_sems,
):
    rows, width = wide.shape[0], packed.shape[1]
    odd = parity()
    own = slice(0, rows)
    sources = [
        (hidden.at[0], wide),
        (table, angles),
        (docs, doc_row),
        (scored, scored_row),
        (
            queries.at[0, :, pl.ds(pl.multiple_of((1 - odd) * GROUP_WIDTH, GROUP_WIDTH), GROUP_WIDTH)],
            swap_out.at[pl.ds(0, rows), pl.ds(PAIR_WIDTH, GROUP_WIDTH)],
        ),
        (queries.at[0, :, pl.ds(width, width)], packed_out.at[pl.ds(0, rows), :]),
    ]
    loads = [
        pltpu.make_async_copy(source, target, in_sems.at[i])
        for i, (source, target) in enumerate(sources)
    ]
    loads[0].start()
    copies = []
    for i, (start, stop) in enumerate(cuts):
        span = pl.ds(start, stop - start)
        copy = pltpu.make_async_copy(weight.at[0, span, :], store.at[span, :], weight_sems.at[i])
        copy.start()
        copies.append(copy)
    for load in loads[1:]:
        load.start()
    results = [
        pltpu.make_async_copy(source, target, out_sems.at[i])
        for i, (source, target) in enumerate(
            (
                (swap_out, swap),
                (away_out, away),
                (mine_out, mine),
                (other_out, other),
                (packed_out, packed),
            )
        )
    ]
    loads[0].wait()
    values = wide[...].astype(jnp.float32)
    scale = lax.rsqrt(jnp.mean(values * values, axis=-1, keepdims=True) + 1e-05)
    normed[...] = (values * scale).astype(jnp.bfloat16)
    for load in loads[1:]:
        load.wait()
    marks = jnp.concatenate([scored_row[...]] * (width // rows), axis=1)
    notes = [doc_row[...], marks, jnp.zeros((NOTE_ROWS - 2, width), jnp.int32)]
    notes = jnp.concatenate(notes, axis=0).astype(jnp.float32).astype(jnp.bfloat16)
    packed_out[rows:, :] = notes
    swap_out[rows:, :] = notes[:, : swap.shape[1]]
    results[4].start()
    base = angles[pl.ds(rows + lax.axis_index("ctx"), 1), :]
    base_cosine, base_sine = base[:, :HEAD_SIZE], base[:, HEAD_SIZE:]
    cosine, sine = angles[own, :HEAD_SIZE], angles[own, HEAD_SIZE:]
    cosine, sine = (
        cosine * base_cosine - sine * base_sine,
        sine * base_cosine + cosine * base_sine,
    )
    sine = jnp.where(lax.broadcasted_iota(jnp.int32, sine.shape, 1) < HEAD_SIZE // 2, -sine, sine)
    total = None
    for copy, (start, stop) in zip(copies, cuts):
        copy.wait()
        part = jnp.dot(
            normed[:, start:stop], store[start:stop, :], preferred_element_type=jnp.float32
        )
        total = part if total is None else total + part
    pairs = []
    for head in range(KEY_VALUE_HEADS):
        key = total[:, head * HEAD_SIZE : (head + 1) * HEAD_SIZE]
        key = key * cosine + pltpu.roll(key, HEAD_SIZE // 2, 1) * sine
        at = (KEY_VALUE_HEADS + head) * HEAD_SIZE
        value = total[:, at : at + HEAD_SIZE]
        pairs.append(jnp.concatenate([key, value], axis=1).astype(jnp.bfloat16))
    for u in range(2):

        @pl.when(odd == u)
        def _():
            mine_out[...] = pairs[u]
            other_out[...] = pairs[1 - u]
            swap_out[own, :PAIR_WIDTH] = pairs[1 - u]

    away_out[:, :PAIR_WIDTH] = pairs[2]
    away_out[:, PAIR_WIDTH:] = pairs[3]
    for result in results[:4]:
        result.start()
    for result in results:
        result.wait()


def project(hidden, weight, queries, docs, scored):
    rows, width = hidden.shape[1], hidden.shape[2]
    columns = weight.shape[2]
    cuts = ((0, width // 2), (width // 2, width))
    table = rotary_table(rows, docs.shape[1] // rows)
    hbm = pl.BlockSpec(memory_space=pltpu.HBM)
    shapes = [
        (rows, PAIR_WIDTH),
        (rows, PAIR_WIDTH),
        (rows + NOTE_ROWS, PAIR_WIDTH + GROUP_WIDTH),
        (rows, 2 * PAIR_WIDTH),
        (rows + NOTE_ROWS, 2 * GROUP_WIDTH),
    ]
    return pl.pallas_call(
        functools.partial(project_kernel, cuts),
        out_shape=[jax.ShapeDtypeStruct(shape, jnp.bfloat16) for shape in shapes],
        in_specs=[hbm] * 6,
        out_specs=[hbm] * 5,
        scratch_shapes=[
            pltpu.VMEM((rows, width), jnp.bfloat16),
            pltpu.VMEM((width, columns), jnp.bfloat16),
            pltpu.VMEM((rows, width), jnp.bfloat16),
            pltpu.VMEM(table.shape, jnp.float32),
            pltpu.VMEM(docs.shape, jnp.int32),
            pltpu.VMEM(scored.shape, jnp.int32),
        ]
        + [pltpu.VMEM(shape, jnp.bfloat16) for shape in shapes]
        + [
            pltpu.SemaphoreType.DMA((6,)),
            pltpu.SemaphoreType.DMA((len(cuts),)),
            pltpu.SemaphoreType.DMA((5,)),
        ],
        compiler_params=pltpu.CompilerParams(vmem_limit_bytes=63 * 2**20),
        cost_estimate=pl.CostEstimate(flops=0, bytes_accessed=0, transcendentals=0),
        name="project",
    )(hidden, weight, queries, table, docs, scored)


def attended(q, keys, values, bias, factor):
    scores = jnp.concatenate(
        [
            lax.dot_general(q, k, (((1,), (1,)), ((), ())), preferred_element_type=jnp.float32)
            for k in keys
        ],
        axis=1,
    )
    scores = scores + bias
    row_max = jnp.max(scores, axis=-1, keepdims=True)
    expo = jnp.exp2((scores - row_max) * factor)
    total = jnp.sum(expo, axis=-1, keepdims=True)
    weights = expo.astype(jnp.bfloat16)
    summed, at = None, 0
    for value in values:
        part = jnp.dot(
            weights[:, at : at + value.shape[0]], value, preferred_element_type=jnp.float32
        )
        summed = part if summed is None else summed + part
        at += value.shape[0]
    return summed / total


def attend_body(q, kvs, doc_row, kept, bias, put):
    rows = q.shape[0]
    place = lax.axis_index("ctx")
    chip, core = place // 2, lax.rem(place, 2)
    cores = (core, 1 - core)

    def docs_of(device):
        row = doc_row(pl.ds(pl.multiple_of(device * rows, rows), rows))
        return jnp.broadcast_to(row.astype(jnp.float32), (rows, rows))

    query_docs = docs_of(place).T
    for back in range(4):
        for b in range(2):
            block = chip - back
            key_docs = docs_of(2 * jnp.maximum(block, 0) + cores[b])
            allowed = query_docs == jnp.where(block >= 0, key_docs, -1.0)
            if back == 0:
                row_at = lax.broadcasted_iota(jnp.int32, (rows, rows), 0)
                key_at = lax.broadcasted_iota(jnp.int32, (rows, rows), 1)
                allowed &= core * rows + row_at >= cores[b] * rows + key_at
            at = (2 * back + b) * rows
            bias[:, at : at + rows] = jnp.where(allowed, 0.0, MASKED)

    kept_rows = jnp.broadcast_to(kept, (rows, rows)).T[:, :1]
    factor = math.log2(math.e) / math.sqrt(HEAD_SIZE)

    def heads(count):
        for head in range(2):
            keys, values = [
                [
                    jnp.concatenate(
                        [kvs[2 * back + b][:, at : at + HEAD_SIZE] for b in range(2)], axis=0
                    )
                    for back in range(count)
                ]
                for at in (head * PAIR_WIDTH, head * PAIR_WIDTH + HEAD_SIZE)
            ]
            for half in range(GROUP // 2):
                at = [(head * GROUP + 2 * half + i) * HEAD_SIZE for i in range(2)]
                pair = jnp.concatenate([q[:, x : x + HEAD_SIZE] for x in at], axis=0)
                mask = bias[:, : 2 * count * rows]
                mask = jnp.concatenate([mask, mask], axis=0)
                result = attended(pair, keys, values, mask, factor)
                for i in range(2):
                    part = result[i * rows : (i + 1) * rows] * kept_rows
                    put(at[i], part.astype(jnp.bfloat16))

    pl.when(chip >= 2)(lambda: heads(4))
    pl.when(chip < 2)(lambda: heads(2))


def attend_home_kernel(
    queries, swap, mine, mine_x, near_x, far, far_x, beyond, beyond_x, docs, scored, out_own, out_other, bias
):
    rows = queries.shape[1]
    place = lax.axis_index("ctx")
    chip, core = place // 2, lax.rem(place, 2)
    partner = place + 2 - 4 * lax.rem(chip, 2)
    behind = place - 4
    crossed = 2 * (3 - chip) + core
    far_off = chip >= 2

    def other_core(device):
        return device + 1 - 2 * lax.rem(device, 2)

    def docs_of(device):
        start = pl.multiple_of(device * rows, rows)
        return jnp.broadcast_to(docs[:, pl.ds(start, rows)].astype(jnp.float32), (rows, rows))

    row_at = lax.broadcasted_iota(jnp.int32, (rows, rows), 0)
    key_at = lax.broadcasted_iota(jnp.int32, (rows, rows), 1)
    sources = []
    for device in (place, partner, behind, crossed):
        device = jnp.where(far_off, device, lax.rem(device + 8, 8))
        sources += [device, other_core(device)]
    query_docs = [docs_of(place).T, docs_of(partner).T]
    for k, device in enumerate(sources):
        key_docs = docs_of(device)
        if k >= 4:
            key_docs = jnp.where(far_off, key_docs, -1.0)
        for a, asker in enumerate((place, partner)):
            allowed = query_docs[a] == key_docs
            if k < 4:
                allowed &= asker * rows + row_at >= device * rows + key_at
            bias[a * rows : (a + 1) * rows, k * rows : (k + 1) * rows] = jnp.where(
                allowed, 0.0, MASKED
            )

    def blocks(at):
        cut = slice(at, at + HEAD_SIZE)
        return [
            jnp.concatenate([one[:rows, cut], twin[:, cut]], axis=0)
            for one, twin in ((mine, mine_x), (swap, near_x), (far, far_x), (beyond, beyond_x))
        ]

    kept = jnp.concatenate(
        [
            jnp.broadcast_to(row, (rows, rows)).T[:, :1]
            for row in (
                scored[...].astype(jnp.float32),
                swap[rows:, :rows].astype(jnp.float32)[1:2],
            )
        ],
        axis=0,
    )
    factor = math.log2(math.e) / math.sqrt(HEAD_SIZE)

    def heads(count):
        keys, values = blocks(0)[:count], blocks(HEAD_SIZE)[:count]
        for head in range(GROUP):
            at = head * HEAD_SIZE
            asked = swap[:rows, PAIR_WIDTH + at : PAIR_WIDTH + at + HEAD_SIZE]
            q = jnp.concatenate([queries[0, :, at : at + HEAD_SIZE], asked], axis=0)
            result = attended(q, keys, values, bias[:, : 2 * count * rows], factor)
            result = (result * kept).astype(jnp.bfloat16)
            out_own[:, at : at + HEAD_SIZE] = result[:rows]
            out_other[:, at : at + HEAD_SIZE] = result[rows:]

    pl.when(far_off)(lambda: heads(4))
    pl.when(jnp.logical_not(far_off))(lambda: heads(2))


class Halves:
    def __init__(self, first, second):
        self.refs = (first, second)
        self.width = first.shape[1]

    def __getitem__(self, index):
        rows, columns = index
        start = columns.start % self.width
        ref = self.refs[columns.start // self.width]
        return ref[rows, start : start + columns.stop - columns.start]


def attend_relayed_kernel(packed, *refs):
    kvs, (out, bias) = refs[:10], refs[10:]
    kvs = kvs[:5] + (Halves(*kvs[5:7]), kvs[7], Halves(*kvs[8:]))
    rows = out.shape[0]
    kept = packed[rows : rows + NOTE_ROWS, :rows].astype(jnp.float32)[1:2]

    def doc_row(at):
        return packed[rows : rows + NOTE_ROWS, at].astype(jnp.float32)[:1]

    def put(at, value):
        out[:, at : at + HEAD_SIZE] = value

    attend_body(packed.at[pl.ds(0, rows), :], kvs, doc_row, kept, bias, put)


def attend_cost(rows, flops):
    return dict(
        scratch_shapes=[pltpu.VMEM((rows, 8 * rows), jnp.float32)],
        compiler_params=pltpu.CompilerParams(vmem_limit_bytes=32 * 2**20),
        cost_estimate=pl.CostEstimate(flops=flops, bytes_accessed=0, transcendentals=0),
    )


def attend_home(queries, *rest):
    rows = queries.shape[1]
    out = jax.ShapeDtypeStruct((rows, GROUP_WIDTH), jnp.bfloat16)

    def whole(array):
        return pl.BlockSpec(array.shape, lambda i: (0,) * array.ndim)

    cost = attend_cost(rows, HOME_FLOPS)
    cost["scratch_shapes"] = [pltpu.VMEM((2 * rows, 8 * rows), jnp.float32)]
    return pl.pallas_call(
        attend_home_kernel,
        grid=(1,),
        out_shape=(out, out),
        in_specs=[pl.BlockSpec((1, rows, GROUP_WIDTH), lambda i: (0, 0, parity()))]
        + [whole(x) for x in rest],
        out_specs=(pl.BlockSpec((rows, GROUP_WIDTH), lambda i: (0, 0)),) * 2,
        name="attend_home",
        **cost,
    )(queries, *rest)


def attend_relayed(packed, kvs):
    rows, width = kvs[0].shape[0], packed.shape[1]
    vmem = pl.BlockSpec(memory_space=pltpu.VMEM)
    return pl.pallas_call(
        attend_relayed_kernel,
        out_shape=jax.ShapeDtypeStruct((rows, width), jnp.bfloat16),
        in_specs=[vmem] * 11,
        out_specs=vmem,
        name="attend_relayed",
        **attend_cost(rows, RELAYED_FLOPS),
    )(packed, *kvs)


def send(block, route):
    pairs = [(2 * a + core, 2 * b + core) for a, b in route for core in range(2)]
    return lax.ppermute(block, "ctx", pairs)


def across(block):
    return lax.ppermute(block, "ctx", [(i, i ^ 1) for i in range(lax.axis_size("ctx"))])


def onward(block, change=0):
    sections, count = lax.axis_size("phase"), lax.axis_size("ctx")
    route = [
        (p * count + c, (p + 1) % sections * count + (c ^ change))
        for p in range(sections)
        for c in range(count)
    ]
    return lax.ppermute(block, ("phase", "ctx"), route)


HOME_FLOPS = int(1.9 * 10**9)
RELAYED_FLOPS = 0


def after(block, *others):
    return lax.optimization_barrier((block,) + others)[0]


def across_halves(block):
    half = block.shape[1] // 2
    return across(block[:, :half]), across(block[:, half:])


def paired(hidden, queries, key_value_weight, doc_ids, scored):
    mine, other, swap, away, packed = project(hidden, key_value_weight, queries, doc_ids, scored)
    away = onward(away)
    swap = send(swap, ((0, 1), (1, 0), (2, 3), (3, 2)))
    far = send(mine, ((0, 2), (1, 3)))
    beyond = send(other, ((0, 3), (1, 2)))
    packed = onward(packed)
    away_1 = send(away, ((0, 1), (1, 2), (2, 3)))
    away_2 = send(away_1, ((1, 2), (2, 3)))
    away_3 = send(away_1, ((1, 3),))
    swap, far, beyond = lax.optimization_barrier((swap, far, beyond))
    mine_x = across(mine)
    own, partners = attend_home(
        queries,
        swap,
        across(mine_x),
        mine_x,
        across(swap[: mine.shape[0], :PAIR_WIDTH]),
        far,
        across(far),
        beyond,
        across(beyond),
        doc_ids,
        scored,
    )
    own, partners = onward(own), onward(partners, 2)
    away = [away, across(away), away_1, across(after(away_1, packed))] + [
        x for block in (away_2, away_3) for x in (block, *across_halves(block))
    ]
    last = attend_relayed(packed, away)
    straight = jnp.concatenate([own, partners, last], axis=1)
    crossed = jnp.concatenate([partners, own, last], axis=1)
    return jnp.where(parity() == 1, crossed, straight)[None]


def solution(mesh):
    placed = (
        P("phase", "ctx", None),
        P("phase", "ctx", None),
        P("phase", None, None),
        P("phase", None),
        P("phase", "ctx"),
    )
    plan = paired if mesh.shape["ctx"] == 8 else gathered_everywhere
    return jax.shard_map(
        plan, mesh=mesh, in_specs=placed, out_specs=P("phase", "ctx", None), check_vma=False
    )
```

```python
import functools
import math

import jax
import jax.numpy as jnp
import numpy as np
from jax import lax
from jax.experimental import pallas as pl
from jax.experimental.pallas import tpu as pltpu
from jax.sharding import PartitionSpec as P

QUERY_HEADS = 16
KEY_VALUE_HEADS = 4
HEAD_SIZE = 128
GROUP = QUERY_HEADS // KEY_VALUE_HEADS
GROUP_WIDTH = GROUP * HEAD_SIZE
PAIR_WIDTH = 2 * HEAD_SIZE
MASKED = -1e30
NOTE_ROWS = 16

rope_base = 500000.0


def from_behind(block, axis, distance):
    devices = range(lax.axis_size(axis))
    route = [((i - distance) % len(devices), i) for i in devices]
    return lax.ppermute(block, axis, route)


def apply_rotary(key_heads, token_positions):
    half_dim = key_heads.shape[-1] // 2
    frequency = rope_base ** (-jnp.arange(half_dim, dtype=jnp.float32) * 2.0 / key_heads.shape[-1])
    angles = token_positions.astype(jnp.float32)[:, None] * frequency[None, :]
    cosine_part = jnp.cos(angles)[:, None, :]
    sine_part = jnp.sin(angles)[:, None, :]
    lower_half = key_heads[..., :half_dim]
    upper_half = key_heads[..., half_dim:]
    return jnp.concatenate(
        [
            lower_half * cosine_part - upper_half * sine_part,
            upper_half * cosine_part + lower_half * sine_part,
        ],
        axis=-1,
    )


def gathered_everywhere(hidden, queries, key_value_weight, doc_ids, scored):
    count_of_rows = hidden.shape[1]
    first_row = lax.axis_index("ctx") * count_of_rows
    token_positions = first_row + jnp.arange(count_of_rows, dtype=jnp.int32)
    wide = hidden[0].astype(jnp.float32)
    normed = (wide * lax.rsqrt(jnp.mean(wide * wide, axis=-1, keepdims=True) + 1e-05)).astype(
        jnp.bfloat16
    )
    projected_rows = jnp.dot(normed, key_value_weight[0], preferred_element_type=jnp.float32)
    key_value_width = KEY_VALUE_HEADS * HEAD_SIZE
    key_matrix = (
        apply_rotary(
            projected_rows[:, :key_value_width].reshape(count_of_rows, KEY_VALUE_HEADS, HEAD_SIZE),
            token_positions,
        )
        .astype(jnp.bfloat16)
        .reshape(count_of_rows, key_value_width)
    )
    value_matrix = projected_rows[:, key_value_width:].astype(jnp.bfloat16)
    query_head_count = queries[0].reshape(count_of_rows, KEY_VALUE_HEADS, GROUP, HEAD_SIZE)
    sequence_docs = doc_ids[0]
    own_docs = lax.dynamic_slice_in_dim(sequence_docs, first_row, count_of_rows, 0)
    score_scale = 1.0 / math.sqrt(HEAD_SIZE)
    stacked = jnp.concatenate([key_matrix, value_matrix], axis=1)
    collected_rows = lax.all_gather(stacked, "ctx", axis=0, tiled=True)
    sequence_length = collected_rows.shape[0]
    every_key_row = collected_rows[:, :key_value_width].reshape(
        sequence_length, KEY_VALUE_HEADS, HEAD_SIZE
    )
    every_value_row = collected_rows[:, key_value_width:].reshape(
        sequence_length, KEY_VALUE_HEADS, HEAD_SIZE
    )
    head_outputs = []
    for key_value_head in range(KEY_VALUE_HEADS):
        key_part = every_key_row[:, key_value_head : key_value_head + 1]
        key_count = key_part.shape[0]
        scores = (
            jnp.einsum(
                "qhgd,khd->hgqk",
                query_head_count[:, key_value_head : key_value_head + 1],
                key_part,
                preferred_element_type=jnp.float32,
            )
            * score_scale
        )
        key_pos = jnp.arange(key_count, dtype=jnp.int32)
        allowed = (key_pos[None, :] <= token_positions[:, None]) & (
            sequence_docs[None, :] == own_docs[:, None]
        )
        scores = jnp.where(allowed[None, None], scores, jnp.float32(MASKED))
        row_max = jnp.max(scores, axis=-1, keepdims=True)
        expo = jnp.exp(scores - row_max)
        total = jnp.sum(expo, axis=-1)
        weights = expo.astype(jnp.bfloat16)
        summed = jnp.einsum(
            "hgqk,khd->hgqd",
            weights,
            every_value_row[:, key_value_head : key_value_head + 1],
            preferred_element_type=jnp.float32,
        )
        head_outputs.append(summed / total[..., None])
    attended = jnp.transpose(jnp.concatenate(head_outputs, axis=0), (2, 0, 1, 3))
    flat = (
        attended.reshape(count_of_rows, QUERY_HEADS * HEAD_SIZE)
        * scored[0].astype(jnp.float32)[:, None]
    )
    outgoing = flat.astype(jnp.bfloat16)[None]
    return from_behind(outgoing, "phase", 1)


def rotary_table(rows, devices):
    half = HEAD_SIZE // 2
    frequency = (rope_base ** (-np.arange(half) * 2.0 / HEAD_SIZE)).astype(np.float32).astype(np.float64)
    frequency = np.concatenate([frequency, frequency])[None, :]
    angles = np.concatenate([np.arange(rows), rows * np.arange(devices)])[:, None] * frequency
    return jnp.asarray(np.concatenate([np.cos(angles), np.sin(angles)], axis=1), jnp.float32)


def parity():
    return lax.rem(lax.axis_index("ctx") // 2, 2)


def project_kernel(
    cuts,
    hidden,
    weight,
    queries,
    table,
    docs,
    scored,
    mine,
    other,
    swap,
    away,
    packed,
    wide,
    store,
    normed,
    angles,
    doc_row,
    scored_row,
    mine_out,
    other_out,
    swap_out,
    away_out,
    packed_out,
    in_sems,
    weight_sems,
    out_sems,
):
    rows, width = wide.shape[0], packed.shape[1]
    odd = parity()
    own = slice(0, rows)
    sources = [
        (hidden.at[0], wide),
        (table, angles),
        (docs, doc_row),
        (scored, scored_row),
        (
            queries.at[0, :, pl.ds(pl.multiple_of((1 - odd) * GROUP_WIDTH, GROUP_WIDTH), GROUP_WIDTH)],
            swap_out.at[pl.ds(0, rows), pl.ds(PAIR_WIDTH, GROUP_WIDTH)],
        ),
        (queries.at[0, :, pl.ds(width, width)], packed_out.at[pl.ds(0, rows), :]),
    ]
    loads = [
        pltpu.make_async_copy(source, target, in_sems.at[i])
        for i, (source, target) in enumerate(sources)
    ]
    loads[0].start()
    copies = []
    for i, (start, stop) in enumerate(cuts):
        span = pl.ds(start, stop - start)
        copies.append(
            pltpu.make_async_copy(weight.at[0, span, :], store.at[span, :], weight_sems.at[i])
        )
    for copy in copies[:2]:
        copy.start()
    for load in loads[1:]:
        load.start()
    results = [
        pltpu.make_async_copy(source, target, out_sems.at[i])
        for i, (source, target) in enumerate(
            (
                (swap_out, swap),
                (away_out, away),
                (mine_out, mine),
                (other_out, other),
                (packed_out, packed),
            )
        )
    ]
    loads[0].wait()
    for copy in copies[2:3]:
        copy.start()
    values = wide[...].astype(jnp.float32)
    scale = lax.rsqrt(jnp.mean(values * values, axis=-1, keepdims=True) + 1e-05)
    normed[...] = (values * scale).astype(jnp.bfloat16)
    for load in loads[1:]:
        load.wait()
    marks = jnp.concatenate([scored_row[...]] * (width // rows), axis=1)
    notes = [doc_row[...], marks, jnp.zeros((NOTE_ROWS - 2, width), jnp.int32)]
    notes = jnp.concatenate(notes, axis=0).astype(jnp.float32).astype(jnp.bfloat16)
    packed_out[rows:, :] = notes
    swap_out[rows:, :] = notes[:, : swap.shape[1]]
    results[4].start()
    base = angles[pl.ds(rows + lax.axis_index("ctx"), 1), :]
    base_cosine, base_sine = base[:, :HEAD_SIZE], base[:, HEAD_SIZE:]
    cosine, sine = angles[own, :HEAD_SIZE], angles[own, HEAD_SIZE:]
    cosine, sine = (
        cosine * base_cosine - sine * base_sine,
        sine * base_cosine + cosine * base_sine,
    )
    sine = jnp.where(lax.broadcasted_iota(jnp.int32, sine.shape, 1) < HEAD_SIZE // 2, -sine, sine)
    total = None
    for i, (start, stop) in enumerate(cuts):
        copies[i].wait()
        if i + 3 < len(copies):
            copies[i + 3].start()
        part = jnp.dot(
            normed[:, start:stop], store[start:stop, :], preferred_element_type=jnp.float32
        )
        total = part if total is None else total + part
    pairs = []
    for head in range(KEY_VALUE_HEADS):
        key = total[:, head * HEAD_SIZE : (head + 1) * HEAD_SIZE]
        key = key * cosine + pltpu.roll(key, HEAD_SIZE // 2, 1) * sine
        at = (KEY_VALUE_HEADS + head) * HEAD_SIZE
        value = total[:, at : at + HEAD_SIZE]
        pairs.append(jnp.concatenate([key, value], axis=1).astype(jnp.bfloat16))
    for u in range(2):

        @pl.when(odd == u)
        def _():
            mine_out[...] = pairs[u]
            other_out[...] = pairs[1 - u]
            swap_out[own, :PAIR_WIDTH] = pairs[1 - u]

    away_out[:, :PAIR_WIDTH] = pairs[2]
    away_out[:, PAIR_WIDTH:] = pairs[3]
    for result in results[:4]:
        result.start()
    for result in results:
        result.wait()


def project(hidden, weight, queries, docs, scored):
    rows, width = hidden.shape[1], hidden.shape[2]
    columns = weight.shape[2]
    edges = [width * x // 16 for x in [0, 5, 10, 14, 16]]
    cuts = tuple(zip(edges[:-1], edges[1:]))
    table = rotary_table(rows, docs.shape[1] // rows)
    hbm = pl.BlockSpec(memory_space=pltpu.HBM)
    shapes = [
        (rows, PAIR_WIDTH),
        (rows, PAIR_WIDTH),
        (rows + NOTE_ROWS, PAIR_WIDTH + GROUP_WIDTH),
        (rows, 2 * PAIR_WIDTH),
        (rows + NOTE_ROWS, 2 * GROUP_WIDTH),
    ]
    return pl.pallas_call(
        functools.partial(project_kernel, cuts),
        out_shape=[jax.ShapeDtypeStruct(shape, jnp.bfloat16) for shape in shapes],
        in_specs=[hbm] * 6,
        out_specs=[hbm] * 5,
        scratch_shapes=[
            pltpu.VMEM((rows, width), jnp.bfloat16),
            pltpu.VMEM((width, columns), jnp.bfloat16),
            pltpu.VMEM((rows, width), jnp.bfloat16),
            pltpu.VMEM(table.shape, jnp.float32),
            pltpu.VMEM(docs.shape, jnp.int32),
            pltpu.VMEM(scored.shape, jnp.int32),
        ]
        + [pltpu.VMEM(shape, jnp.bfloat16) for shape in shapes]
        + [
            pltpu.SemaphoreType.DMA((6,)),
            pltpu.SemaphoreType.DMA((len(cuts),)),
            pltpu.SemaphoreType.DMA((5,)),
        ],
        compiler_params=pltpu.CompilerParams(vmem_limit_bytes=63 * 2**20),
        cost_estimate=pl.CostEstimate(flops=0, bytes_accessed=0, transcendentals=0),
        name="project",
    )(hidden, weight, queries, table, docs, scored)


def attended(q, keys, values, bias, factor):
    scores = jnp.concatenate(
        [
            lax.dot_general(q, k, (((1,), (1,)), ((), ())), preferred_element_type=jnp.float32)
            for k in keys
        ],
        axis=1,
    )
    scores = scores + bias
    row_max = jnp.max(scores, axis=-1, keepdims=True)
    expo = jnp.exp2((scores - row_max) * factor)
    total = jnp.sum(expo, axis=-1, keepdims=True)
    weights = expo.astype(jnp.bfloat16)
    summed, at = None, 0
    for value in values:
        part = jnp.dot(
            weights[:, at : at + value.shape[0]], value, preferred_element_type=jnp.float32
        )
        summed = part if summed is None else summed + part
        at += value.shape[0]
    return summed / total


def attend_body(q, kvs, doc_row, kept, bias, put):
    rows = q.shape[0]
    place = lax.axis_index("ctx")
    chip, core = place // 2, lax.rem(place, 2)
    cores = (core, 1 - core)

    def docs_of(device):
        row = doc_row(pl.ds(pl.multiple_of(device * rows, rows), rows))
        return jnp.broadcast_to(row.astype(jnp.float32), (rows, rows))

    query_docs = docs_of(place).T
    for back in range(4):
        for b in range(2):
            block = chip - back
            key_docs = docs_of(2 * jnp.maximum(block, 0) + cores[b])
            allowed = query_docs == jnp.where(block >= 0, key_docs, -1.0)
            if back == 0:
                row_at = lax.broadcasted_iota(jnp.int32, (rows, rows), 0)
                key_at = lax.broadcasted_iota(jnp.int32, (rows, rows), 1)
                allowed &= core * rows + row_at >= cores[b] * rows + key_at
            at = (2 * back + b) * rows
            bias[:, at : at + rows] = jnp.where(allowed, 0.0, MASKED)

    kept_rows = jnp.broadcast_to(kept, (rows, rows)).T[:, :1]
    factor = math.log2(math.e) / math.sqrt(HEAD_SIZE)

    def heads(count):
        for head in range(2):
            keys, values = [
                [
                    jnp.concatenate(
                        [kvs[2 * back + b][:, at : at + HEAD_SIZE] for b in range(2)], axis=0
                    )
                    for back in range(count)
                ]
                for at in (head * PAIR_WIDTH, head * PAIR_WIDTH + HEAD_SIZE)
            ]
            for half in range(GROUP // 2):
                at = [(head * GROUP + 2 * half + i) * HEAD_SIZE for i in range(2)]
                pair = jnp.concatenate([q[:, x : x + HEAD_SIZE] for x in at], axis=0)
                mask = bias[:, : 2 * count * rows]
                mask = jnp.concatenate([mask, mask], axis=0)
                result = attended(pair, keys, values, mask, factor)
                for i in range(2):
                    part = result[i * rows : (i + 1) * rows] * kept_rows
                    put(at[i], part.astype(jnp.bfloat16))

    pl.when(chip >= 2)(lambda: heads(4))
    pl.when(chip < 2)(lambda: heads(2))


def attend_home_kernel(
    queries, swap, mine, mine_x, near_x, far, far_x, beyond, beyond_x, docs, scored, out_own, out_other, bias
):
    rows = queries.shape[1]
    place = lax.axis_index("ctx")
    chip, core = place // 2, lax.rem(place, 2)
    partner = place + 2 - 4 * lax.rem(chip, 2)
    behind = place - 4
    crossed = 2 * (3 - chip) + core
    far_off = chip >= 2

    def other_core(device):
        return device + 1 - 2 * lax.rem(device, 2)

    def docs_of(device):
        start = pl.multiple_of(device * rows, rows)
        return jnp.broadcast_to(docs[:, pl.ds(start, rows)].astype(jnp.float32), (rows, rows))

    row_at = lax.broadcasted_iota(jnp.int32, (rows, rows), 0)
    key_at = lax.broadcasted_iota(jnp.int32, (rows, rows), 1)
    sources = []
    for device in (place, partner, behind, crossed):
        device = jnp.where(far_off, device, lax.rem(device + 8, 8))
        sources += [device, other_core(device)]
    query_docs = [docs_of(place).T, docs_of(partner).T]
    for k, device in enumerate(sources):
        key_docs = docs_of(device)
        if k >= 4:
            key_docs = jnp.where(far_off, key_docs, -1.0)
        for a, asker in enumerate((place, partner)):
            allowed = query_docs[a] == key_docs
            if k < 4:
                allowed &= asker * rows + row_at >= device * rows + key_at
            bias[a * rows : (a + 1) * rows, k * rows : (k + 1) * rows] = jnp.where(
                allowed, 0.0, MASKED
            )

    def blocks(at):
        cut = slice(at, at + HEAD_SIZE)
        return [
            jnp.concatenate([one[:rows, cut], twin[:, cut]], axis=0)
            for one, twin in ((mine, mine_x), (swap, near_x), (far, far_x), (beyond, beyond_x))
        ]

    kept = jnp.concatenate(
        [
            jnp.broadcast_to(row, (rows, rows)).T[:, :1]
            for row in (
                scored[...].astype(jnp.float32),
                swap[rows:, :rows].astype(jnp.float32)[1:2],
            )
        ],
        axis=0,
    )
    factor = math.log2(math.e) / math.sqrt(HEAD_SIZE)

    def heads(count):
        keys, values = blocks(0)[:count], blocks(HEAD_SIZE)[:count]
        for head in range(GROUP):
            at = head * HEAD_SIZE
            asked = swap[:rows, PAIR_WIDTH + at : PAIR_WIDTH + at + HEAD_SIZE]
            q = jnp.concatenate([queries[0, :, at : at + HEAD_SIZE], asked], axis=0)
            result = attended(q, keys, values, bias[:, : 2 * count * rows], factor)
            result = (result * kept).astype(jnp.bfloat16)
            out_own[:, at : at + HEAD_SIZE] = result[:rows]
            out_other[:, at : at + HEAD_SIZE] = result[rows:]

    pl.when(far_off)(lambda: heads(4))
    pl.when(jnp.logical_not(far_off))(lambda: heads(2))


class Halves:
    def __init__(self, first, second):
        self.refs = (first, second)
        self.width = first.shape[1]

    def __getitem__(self, index):
        rows, columns = index
        start = columns.start % self.width
        ref = self.refs[columns.start // self.width]
        return ref[rows, start : start + columns.stop - columns.start]


def attend_relayed_kernel(packed, *refs):
    kvs, (out, bias) = refs[:10], refs[10:]
    kvs = kvs[:5] + (Halves(*kvs[5:7]), kvs[7], Halves(*kvs[8:]))
    rows = out.shape[0]
    kept = packed[rows : rows + NOTE_ROWS, :rows].astype(jnp.float32)[1:2]

    def doc_row(at):
        return packed[rows : rows + NOTE_ROWS, at].astype(jnp.float32)[:1]

    def put(at, value):
        out[:, at : at + HEAD_SIZE] = value

    attend_body(packed.at[pl.ds(0, rows), :], kvs, doc_row, kept, bias, put)


def attend_cost(rows, flops):
    return dict(
        scratch_shapes=[pltpu.VMEM((rows, 8 * rows), jnp.float32)],
        compiler_params=pltpu.CompilerParams(vmem_limit_bytes=32 * 2**20),
        cost_estimate=pl.CostEstimate(flops=flops, bytes_accessed=0, transcendentals=0),
    )


def attend_home(queries, *rest):
    rows = queries.shape[1]
    out = jax.ShapeDtypeStruct((rows, GROUP_WIDTH), jnp.bfloat16)

    def whole(array):
        return pl.BlockSpec(array.shape, lambda i: (0,) * array.ndim)

    cost = attend_cost(rows, HOME_FLOPS)
    cost["scratch_shapes"] = [pltpu.VMEM((2 * rows, 8 * rows), jnp.float32)]
    return pl.pallas_call(
        attend_home_kernel,
        grid=(1,),
        out_shape=(out, out),
        in_specs=[pl.BlockSpec((1, rows, GROUP_WIDTH), lambda i: (0, 0, parity()))]
        + [whole(x) for x in rest],
        out_specs=(pl.BlockSpec((rows, GROUP_WIDTH), lambda i: (0, 0)),) * 2,
        name="attend_home",
        **cost,
    )(queries, *rest)


def attend_relayed(packed, kvs):
    rows, width = kvs[0].shape[0], packed.shape[1]
    vmem = pl.BlockSpec(memory_space=pltpu.VMEM)
    return pl.pallas_call(
        attend_relayed_kernel,
        out_shape=jax.ShapeDtypeStruct((rows, width), jnp.bfloat16),
        in_specs=[vmem] * 11,
        out_specs=vmem,
        name="attend_relayed",
        **attend_cost(rows, RELAYED_FLOPS),
    )(packed, *kvs)


def send(block, route):
    pairs = [(2 * a + core, 2 * b + core) for a, b in route for core in range(2)]
    return lax.ppermute(block, "ctx", pairs)


def across(block):
    return lax.ppermute(block, "ctx", [(i, i ^ 1) for i in range(lax.axis_size("ctx"))])


def onward(block, change=0):
    sections, count = lax.axis_size("phase"), lax.axis_size("ctx")
    route = [
        (p * count + c, (p + 1) % sections * count + (c ^ change))
        for p in range(sections)
        for c in range(count)
    ]
    return lax.ppermute(block, ("phase", "ctx"), route)


HOME_FLOPS = int(1.9 * 10**9)
RELAYED_FLOPS = 0


def after(block, *others):
    return lax.optimization_barrier((block,) + others)[0]


def across_halves(block):
    half = block.shape[1] // 2
    return across(block[:, :half]), across(block[:, half:])


def paired(hidden, queries, key_value_weight, doc_ids, scored):
    mine, other, swap, away, packed = project(hidden, key_value_weight, queries, doc_ids, scored)
    away = onward(away)
    swap = send(swap, ((0, 1), (1, 0), (2, 3), (3, 2)))
    far = send(mine, ((0, 2), (1, 3)))
    beyond = send(other, ((0, 3), (1, 2)))
    packed = onward(packed)
    away_1 = send(away, ((0, 1), (1, 2), (2, 3)))
    away_2 = send(away_1, ((1, 2), (2, 3)))
    away_3 = send(away_1, ((1, 3),))
    swap, far, beyond = lax.optimization_barrier((swap, far, beyond))
    mine_x = across(mine)
    own, partners = attend_home(
        queries,
        swap,
        across(mine_x),
        mine_x,
        across(swap[: mine.shape[0], :PAIR_WIDTH]),
        far,
        across(far),
        beyond,
        across(beyond),
        doc_ids,
        scored,
    )
    own, partners = onward(own), onward(partners, 2)
    away = [away, across(away), away_1, across(after(away_1, packed))] + [
        x for block in (away_2, away_3) for x in (block, *across_halves(block))
    ]
    last = attend_relayed(packed, away)
    straight = jnp.concatenate([own, partners, last], axis=1)
    crossed = jnp.concatenate([partners, own, last], axis=1)
    return jnp.where(parity() == 1, crossed, straight)[None]


def solution(mesh):
    placed = (
        P("phase", "ctx", None),
        P("phase", "ctx", None),
        P("phase", None, None),
        P("phase", None),
        P("phase", "ctx"),
    )
    plan = paired if mesh.shape["ctx"] == 8 else gathered_everywhere
    return jax.shard_map(
        plan, mesh=mesh, in_specs=placed, out_specs=P("phase", "ctx", None), check_vma=False
    )
```

```python
import functools
import math

import jax
import jax.numpy as jnp
import numpy as np
from jax import lax
from jax.experimental import pallas as pl
from jax.experimental.pallas import tpu as pltpu
from jax.sharding import PartitionSpec as P

QUERY_HEADS = 16
KEY_VALUE_HEADS = 4
HEAD_SIZE = 128
GROUP = QUERY_HEADS // KEY_VALUE_HEADS
GROUP_WIDTH = GROUP * HEAD_SIZE
PAIR_WIDTH = 2 * HEAD_SIZE
MASKED = -1e30
NOTE_ROWS = 16

rope_base = 500000.0


def from_behind(block, axis, distance):
    devices = range(lax.axis_size(axis))
    route = [((i - distance) % len(devices), i) for i in devices]
    return lax.ppermute(block, axis, route)


def apply_rotary(key_heads, token_positions):
    half_dim = key_heads.shape[-1] // 2
    frequency = rope_base ** (-jnp.arange(half_dim, dtype=jnp.float32) * 2.0 / key_heads.shape[-1])
    angles = token_positions.astype(jnp.float32)[:, None] * frequency[None, :]
    cosine_part = jnp.cos(angles)[:, None, :]
    sine_part = jnp.sin(angles)[:, None, :]
    lower_half = key_heads[..., :half_dim]
    upper_half = key_heads[..., half_dim:]
    return jnp.concatenate(
        [
            lower_half * cosine_part - upper_half * sine_part,
            upper_half * cosine_part + lower_half * sine_part,
        ],
        axis=-1,
    )


def gathered_everywhere(hidden, queries, key_value_weight, doc_ids, scored):
    count_of_rows = hidden.shape[1]
    first_row = lax.axis_index("ctx") * count_of_rows
    token_positions = first_row + jnp.arange(count_of_rows, dtype=jnp.int32)
    wide = hidden[0].astype(jnp.float32)
    normed = (wide * lax.rsqrt(jnp.mean(wide * wide, axis=-1, keepdims=True) + 1e-05)).astype(
        jnp.bfloat16
    )
    projected_rows = jnp.dot(normed, key_value_weight[0], preferred_element_type=jnp.float32)
    key_value_width = KEY_VALUE_HEADS * HEAD_SIZE
    key_matrix = (
        apply_rotary(
            projected_rows[:, :key_value_width].reshape(count_of_rows, KEY_VALUE_HEADS, HEAD_SIZE),
            token_positions,
        )
        .astype(jnp.bfloat16)
        .reshape(count_of_rows, key_value_width)
    )
    value_matrix = projected_rows[:, key_value_width:].astype(jnp.bfloat16)
    query_head_count = queries[0].reshape(count_of_rows, KEY_VALUE_HEADS, GROUP, HEAD_SIZE)
    sequence_docs = doc_ids[0]
    own_docs = lax.dynamic_slice_in_dim(sequence_docs, first_row, count_of_rows, 0)
    score_scale = 1.0 / math.sqrt(HEAD_SIZE)
    stacked = jnp.concatenate([key_matrix, value_matrix], axis=1)
    collected_rows = lax.all_gather(stacked, "ctx", axis=0, tiled=True)
    sequence_length = collected_rows.shape[0]
    every_key_row = collected_rows[:, :key_value_width].reshape(
        sequence_length, KEY_VALUE_HEADS, HEAD_SIZE
    )
    every_value_row = collected_rows[:, key_value_width:].reshape(
        sequence_length, KEY_VALUE_HEADS, HEAD_SIZE
    )
    head_outputs = []
    for key_value_head in range(KEY_VALUE_HEADS):
        key_part = every_key_row[:, key_value_head : key_value_head + 1]
        key_count = key_part.shape[0]
        scores = (
            jnp.einsum(
                "qhgd,khd->hgqk",
                query_head_count[:, key_value_head : key_value_head + 1],
                key_part,
                preferred_element_type=jnp.float32,
            )
            * score_scale
        )
        key_pos = jnp.arange(key_count, dtype=jnp.int32)
        allowed = (key_pos[None, :] <= token_positions[:, None]) & (
            sequence_docs[None, :] == own_docs[:, None]
        )
        scores = jnp.where(allowed[None, None], scores, jnp.float32(MASKED))
        row_max = jnp.max(scores, axis=-1, keepdims=True)
        expo = jnp.exp(scores - row_max)
        total = jnp.sum(expo, axis=-1)
        weights = expo.astype(jnp.bfloat16)
        summed = jnp.einsum(
            "hgqk,khd->hgqd",
            weights,
            every_value_row[:, key_value_head : key_value_head + 1],
            preferred_element_type=jnp.float32,
        )
        head_outputs.append(summed / total[..., None])
    attended = jnp.transpose(jnp.concatenate(head_outputs, axis=0), (2, 0, 1, 3))
    flat = (
        attended.reshape(count_of_rows, QUERY_HEADS * HEAD_SIZE)
        * scored[0].astype(jnp.float32)[:, None]
    )
    outgoing = flat.astype(jnp.bfloat16)[None]
    return from_behind(outgoing, "phase", 1)


def rotary_table(rows, devices):
    half = HEAD_SIZE // 2
    frequency = (rope_base ** (-np.arange(half) * 2.0 / HEAD_SIZE)).astype(np.float32).astype(np.float64)
    frequency = np.concatenate([frequency, frequency])[None, :]
    angles = np.concatenate([np.arange(rows), rows * np.arange(devices)])[:, None] * frequency
    return jnp.asarray(np.concatenate([np.cos(angles), np.sin(angles)], axis=1), jnp.float32)


def parity():
    return lax.rem(lax.axis_index("ctx") // 2, 2)


def project_kernel(
    cuts,
    hidden,
    weight,
    queries,
    table,
    docs,
    scored,
    mine,
    other,
    swap,
    away,
    packed,
    wide,
    store,
    normed,
    angles,
    doc_row,
    scored_row,
    mine_out,
    other_out,
    swap_out,
    away_out,
    packed_out,
    in_sems,
    weight_sems,
    out_sems,
):
    rows, width = wide.shape[0], packed.shape[1]
    odd = parity()
    own = slice(0, rows)
    sources = [
        (hidden.at[0], wide),
        (table, angles),
        (docs, doc_row),
        (scored, scored_row),
        (
            queries.at[0, :, pl.ds(pl.multiple_of((1 - odd) * GROUP_WIDTH, GROUP_WIDTH), GROUP_WIDTH)],
            swap_out.at[pl.ds(0, rows), pl.ds(PAIR_WIDTH, GROUP_WIDTH)],
        ),
        (queries.at[0, :, pl.ds(width, width)], packed_out.at[pl.ds(0, rows), :]),
    ]
    loads = [
        pltpu.make_async_copy(source, target, in_sems.at[i])
        for i, (source, target) in enumerate(sources)
    ]
    loads[0].start()
    copies = []
    for i, (start, stop) in enumerate(cuts):
        span = pl.ds(start, stop - start)
        copies.append(
            pltpu.make_async_copy(weight.at[0, span, :], store.at[span, :], weight_sems.at[i])
        )
    for copy in copies[:2]:
        copy.start()
    for load in loads[1:]:
        load.start()
    results = [
        pltpu.make_async_copy(source, target, out_sems.at[i])
        for i, (source, target) in enumerate(
            (
                (swap_out, swap),
                (away_out, away),
                (mine_out, mine),
                (other_out, other),
                (packed_out, packed),
            )
        )
    ]
    loads[0].wait()
    for copy in copies[2:3]:
        copy.start()
    values = wide[...].astype(jnp.float32)
    scale = lax.rsqrt(jnp.mean(values * values, axis=-1, keepdims=True) + 1e-05)
    normed[...] = (values * scale).astype(jnp.bfloat16)
    for load in loads[1:]:
        load.wait()
    marks = jnp.concatenate([scored_row[...]] * (width // rows), axis=1)
    notes = [doc_row[...], marks, jnp.zeros((NOTE_ROWS - 2, width), jnp.int32)]
    notes = jnp.concatenate(notes, axis=0).astype(jnp.float32).astype(jnp.bfloat16)
    packed_out[rows:, :] = notes
    swap_out[rows:, :] = notes[:, : swap.shape[1]]
    results[4].start()
    base = angles[pl.ds(rows + lax.axis_index("ctx"), 1), :]
    base_cosine, base_sine = base[:, :HEAD_SIZE], base[:, HEAD_SIZE:]
    cosine, sine = angles[own, :HEAD_SIZE], angles[own, HEAD_SIZE:]
    cosine, sine = (
        cosine * base_cosine - sine * base_sine,
        sine * base_cosine + cosine * base_sine,
    )
    sine = jnp.where(lax.broadcasted_iota(jnp.int32, sine.shape, 1) < HEAD_SIZE // 2, -sine, sine)
    total = None
    for i, (start, stop) in enumerate(cuts):
        copies[i].wait()
        if i + 3 < len(copies):
            copies[i + 3].start()
        part = jnp.dot(
            normed[:, start:stop], store[start:stop, :], preferred_element_type=jnp.float32
        )
        total = part if total is None else total + part
    pairs = []
    for head in range(KEY_VALUE_HEADS):
        key = total[:, head * HEAD_SIZE : (head + 1) * HEAD_SIZE]
        key = key * cosine + pltpu.roll(key, HEAD_SIZE // 2, 1) * sine
        at = (KEY_VALUE_HEADS + head) * HEAD_SIZE
        value = total[:, at : at + HEAD_SIZE]
        pairs.append(jnp.concatenate([key, value], axis=1).astype(jnp.bfloat16))
    for u in range(2):

        @pl.when(odd == u)
        def _():
            mine_out[...] = pairs[u]
            other_out[...] = pairs[1 - u]
            swap_out[own, :PAIR_WIDTH] = pairs[1 - u]

    away_out[:, :PAIR_WIDTH] = pairs[2]
    away_out[:, PAIR_WIDTH:] = pairs[3]
    for result in results[:4]:
        result.start()
    for result in results:
        result.wait()


def project(hidden, weight, queries, docs, scored):
    rows, width = hidden.shape[1], hidden.shape[2]
    columns = weight.shape[2]
    edges = [width * x // 16 for x in [0, 5, 10, 14, 16]]
    cuts = tuple(zip(edges[:-1], edges[1:]))
    table = rotary_table(rows, docs.shape[1] // rows)
    hbm = pl.BlockSpec(memory_space=pltpu.HBM)
    shapes = [
        (rows, PAIR_WIDTH),
        (rows, PAIR_WIDTH),
        (rows + NOTE_ROWS, PAIR_WIDTH + GROUP_WIDTH),
        (rows, 2 * PAIR_WIDTH),
        (rows + NOTE_ROWS, 2 * GROUP_WIDTH),
    ]
    return pl.pallas_call(
        functools.partial(project_kernel, cuts),
        out_shape=[jax.ShapeDtypeStruct(shape, jnp.bfloat16) for shape in shapes],
        in_specs=[hbm] * 6,
        out_specs=[hbm] * 5,
        scratch_shapes=[
            pltpu.VMEM((rows, width), jnp.bfloat16),
            pltpu.VMEM((width, columns), jnp.bfloat16),
            pltpu.VMEM((rows, width), jnp.bfloat16),
            pltpu.VMEM(table.shape, jnp.float32),
            pltpu.VMEM(docs.shape, jnp.int32),
            pltpu.VMEM(scored.shape, jnp.int32),
        ]
        + [pltpu.VMEM(shape, jnp.bfloat16) for shape in shapes]
        + [
            pltpu.SemaphoreType.DMA((6,)),
            pltpu.SemaphoreType.DMA((len(cuts),)),
            pltpu.SemaphoreType.DMA((5,)),
        ],
        compiler_params=pltpu.CompilerParams(vmem_limit_bytes=63 * 2**20),
        cost_estimate=pl.CostEstimate(flops=0, bytes_accessed=0, transcendentals=0),
        name="project",
    )(hidden, weight, queries, table, docs, scored)


def attended(q, keys, values, bias, factor):
    scores = jnp.concatenate(
        [
            lax.dot_general(q, k, (((1,), (1,)), ((), ())), preferred_element_type=jnp.float32)
            for k in keys
        ],
        axis=1,
    )
    scores = scores + bias
    row_max = jnp.max(scores, axis=-1, keepdims=True)
    expo = jnp.exp2((scores - row_max) * factor)
    total = jnp.sum(expo, axis=-1, keepdims=True)
    weights = expo.astype(jnp.bfloat16)
    summed, at = None, 0
    for value in values:
        part = jnp.dot(
            weights[:, at : at + value.shape[0]], value, preferred_element_type=jnp.float32
        )
        summed = part if summed is None else summed + part
        at += value.shape[0]
    return summed / total


def attend_body(q, kvs, doc_row, kept, bias, put):
    rows = q.shape[0]
    place = lax.axis_index("ctx")
    chip, core = place // 2, lax.rem(place, 2)
    cores = (core, 1 - core)

    def docs_of(device):
        row = doc_row(pl.ds(pl.multiple_of(device * rows, rows), rows))
        return jnp.broadcast_to(row.astype(jnp.float32), (rows, rows))

    query_docs = docs_of(place).T
    for back in range(4):
        for b in range(2):
            block = chip - back
            key_docs = docs_of(2 * jnp.maximum(block, 0) + cores[b])
            allowed = query_docs == jnp.where(block >= 0, key_docs, -1.0)
            if back == 0:
                row_at = lax.broadcasted_iota(jnp.int32, (rows, rows), 0)
                key_at = lax.broadcasted_iota(jnp.int32, (rows, rows), 1)
                allowed &= core * rows + row_at >= cores[b] * rows + key_at
            at = (2 * back + b) * rows
            bias[:, at : at + rows] = jnp.where(allowed, 0.0, MASKED)

    kept_rows = jnp.broadcast_to(kept, (rows, rows)).T[:, :1]
    factor = math.log2(math.e) / math.sqrt(HEAD_SIZE)

    def heads(count):
        for head in range(2):
            keys, values = [
                [
                    jnp.concatenate(
                        [kvs[2 * back + b][:, at : at + HEAD_SIZE] for b in range(2)], axis=0
                    )
                    for back in range(count)
                ]
                for at in (head * PAIR_WIDTH, head * PAIR_WIDTH + HEAD_SIZE)
            ]
            for half in range(GROUP // 2):
                at = [(head * GROUP + 2 * half + i) * HEAD_SIZE for i in range(2)]
                pair = jnp.concatenate([q[:, x : x + HEAD_SIZE] for x in at], axis=0)
                mask = bias[:, : 2 * count * rows]
                mask = jnp.concatenate([mask, mask], axis=0)
                result = attended(pair, keys, values, mask, factor)
                for i in range(2):
                    part = result[i * rows : (i + 1) * rows] * kept_rows
                    put(at[i], part.astype(jnp.bfloat16))

    for last in range(4):
        pl.when(chip == last)(functools.partial(heads, last + 1))


def attend_home_kernel(
    queries, swap, mine, mine_x, near_x, far, far_x, beyond, beyond_x, docs, scored, out_own, out_other, bias
):
    rows = queries.shape[1]
    place = lax.axis_index("ctx")
    chip, core = place // 2, lax.rem(place, 2)
    partner = place + 2 - 4 * lax.rem(chip, 2)
    behind = place - 4
    crossed = 2 * (3 - chip) + core
    far_off = chip >= 2

    def other_core(device):
        return device + 1 - 2 * lax.rem(device, 2)

    def docs_of(device):
        start = pl.multiple_of(device * rows, rows)
        return jnp.broadcast_to(docs[:, pl.ds(start, rows)].astype(jnp.float32), (rows, rows))

    row_at = lax.broadcasted_iota(jnp.int32, (rows, rows), 0)
    key_at = lax.broadcasted_iota(jnp.int32, (rows, rows), 1)
    sources = []
    for device in (place, partner, behind, crossed):
        device = jnp.where(far_off, device, lax.rem(device + 8, 8))
        sources += [device, other_core(device)]
    query_docs = [docs_of(place).T, docs_of(partner).T]
    for k, device in enumerate(sources):
        key_docs = docs_of(device)
        if k >= 4:
            key_docs = jnp.where(far_off, key_docs, -1.0)
        for a, asker in enumerate((place, partner)):
            allowed = query_docs[a] == key_docs
            if k < 4:
                allowed &= asker * rows + row_at >= device * rows + key_at
            bias[a * rows : (a + 1) * rows, k * rows : (k + 1) * rows] = jnp.where(
                allowed, 0.0, MASKED
            )

    def blocks(at):
        cut = slice(at, at + HEAD_SIZE)
        return [
            jnp.concatenate([one[:rows, cut], twin[:, cut]], axis=0)
            for one, twin in ((mine, mine_x), (swap, near_x), (far, far_x), (beyond, beyond_x))
        ]

    kept = jnp.concatenate(
        [
            jnp.broadcast_to(row, (rows, rows)).T[:, :1]
            for row in (
                scored[...].astype(jnp.float32),
                swap[rows:, :rows].astype(jnp.float32)[1:2],
            )
        ],
        axis=0,
    )
    factor = math.log2(math.e) / math.sqrt(HEAD_SIZE)

    def heads(count):
        keys, values = blocks(0)[:count], blocks(HEAD_SIZE)[:count]
        for head in range(GROUP):
            at = head * HEAD_SIZE
            asked = swap[:rows, PAIR_WIDTH + at : PAIR_WIDTH + at + HEAD_SIZE]
            q = jnp.concatenate([queries[0, :, at : at + HEAD_SIZE], asked], axis=0)
            result = attended(q, keys, values, bias[:, : 2 * count * rows], factor)
            result = (result * kept).astype(jnp.bfloat16)
            out_own[:, at : at + HEAD_SIZE] = result[:rows]
            out_other[:, at : at + HEAD_SIZE] = result[rows:]

    pl.when(far_off)(lambda: heads(4))
    pl.when(jnp.logical_not(far_off))(lambda: heads(2))


class Halves:
    def __init__(self, first, second):
        self.refs = (first, second)
        self.width = first.shape[1]

    def __getitem__(self, index):
        rows, columns = index
        start = columns.start % self.width
        ref = self.refs[columns.start // self.width]
        return ref[rows, start : start + columns.stop - columns.start]


def attend_relayed_kernel(packed, *refs):
    kvs, (out, bias) = refs[:10], refs[10:]
    kvs = kvs[:5] + (Halves(*kvs[5:7]), kvs[7], Halves(*kvs[8:]))
    rows = out.shape[0]
    kept = packed[rows : rows + NOTE_ROWS, :rows].astype(jnp.float32)[1:2]

    def doc_row(at):
        return packed[rows : rows + NOTE_ROWS, at].astype(jnp.float32)[:1]

    def put(at, value):
        out[:, at : at + HEAD_SIZE] = value

    attend_body(packed.at[pl.ds(0, rows), :], kvs, doc_row, kept, bias, put)


def attend_cost(rows, flops):
    return dict(
        scratch_shapes=[pltpu.VMEM((rows, 8 * rows), jnp.float32)],
        compiler_params=pltpu.CompilerParams(vmem_limit_bytes=32 * 2**20),
        cost_estimate=pl.CostEstimate(flops=flops, bytes_accessed=0, transcendentals=0),
    )


def attend_home(queries, *rest):
    rows = queries.shape[1]
    out = jax.ShapeDtypeStruct((rows, GROUP_WIDTH), jnp.bfloat16)

    def whole(array):
        return pl.BlockSpec(array.shape, lambda i: (0,) * array.ndim)

    cost = attend_cost(rows, HOME_FLOPS)
    cost["scratch_shapes"] = [pltpu.VMEM((2 * rows, 8 * rows), jnp.float32)]
    return pl.pallas_call(
        attend_home_kernel,
        grid=(1,),
        out_shape=(out, out),
        in_specs=[pl.BlockSpec((1, rows, GROUP_WIDTH), lambda i: (0, 0, parity()))]
        + [whole(x) for x in rest],
        out_specs=(pl.BlockSpec((rows, GROUP_WIDTH), lambda i: (0, 0)),) * 2,
        name="attend_home",
        **cost,
    )(queries, *rest)


def attend_relayed(packed, kvs):
    rows, width = kvs[0].shape[0], packed.shape[1]
    vmem = pl.BlockSpec(memory_space=pltpu.VMEM)
    return pl.pallas_call(
        attend_relayed_kernel,
        out_shape=jax.ShapeDtypeStruct((rows, width), jnp.bfloat16),
        in_specs=[vmem] * 11,
        out_specs=vmem,
        name="attend_relayed",
        **attend_cost(rows, RELAYED_FLOPS),
    )(packed, *kvs)


def send(block, route):
    pairs = [(2 * a + core, 2 * b + core) for a, b in route for core in range(2)]
    return lax.ppermute(block, "ctx", pairs)


def across(block):
    return lax.ppermute(block, "ctx", [(i, i ^ 1) for i in range(lax.axis_size("ctx"))])


def onward(block, change=0):
    sections, count = lax.axis_size("phase"), lax.axis_size("ctx")
    route = [
        (p * count + c, (p + 1) % sections * count + (c ^ change))
        for p in range(sections)
        for c in range(count)
    ]
    return lax.ppermute(block, ("phase", "ctx"), route)


HOME_FLOPS = int(1.9 * 10**9)
RELAYED_FLOPS = 0


def after(block, *others):
    return lax.optimization_barrier((block,) + others)[0]


def across_halves(block):
    half = block.shape[1] // 2
    return across(block[:, :half]), across(block[:, half:])


def paired(hidden, queries, key_value_weight, doc_ids, scored):
    mine, other, swap, away, packed = project(hidden, key_value_weight, queries, doc_ids, scored)
    away = onward(away)
    swap = send(swap, ((0, 1), (1, 0), (2, 3), (3, 2)))
    far = send(mine, ((0, 2), (1, 3)))
    beyond = send(other, ((0, 3), (1, 2)))
    packed = onward(packed)
    away_1 = send(away, ((0, 1), (1, 2), (2, 3)))
    away_2 = send(away_1, ((1, 2), (2, 3)))
    away_3 = send(away_1, ((1, 3),))
    swap, far, beyond = lax.optimization_barrier((swap, far, beyond))
    mine_x = across(mine)
    own, partners = attend_home(
        queries,
        swap,
        across(mine_x),
        mine_x,
        across(swap[: mine.shape[0], :PAIR_WIDTH]),
        far,
        across(far),
        beyond,
        across(beyond),
        doc_ids,
        scored,
    )
    own, partners = onward(own), onward(partners, 2)
    away = [away, across(away), away_1, across(after(away_1, packed))] + [
        x for block in (away_2, away_3) for x in (block, *across_halves(block))
    ]
    last = attend_relayed(packed, away)
    crossed = jnp.concatenate([partners, own, last], axis=1)
    straight = jnp.concatenate([own, partners, last], axis=1)
    return jnp.where(parity() == 0, straight, crossed)[None]


def solution(mesh):
    placed = (
        P("phase", "ctx", None),
        P("phase", "ctx", None),
        P("phase", None, None),
        P("phase", None),
        P("phase", "ctx"),
    )
    plan = paired if mesh.shape["ctx"] == 8 else gathered_everywhere
    return jax.shard_map(
        plan, mesh=mesh, in_specs=placed, out_specs=P("phase", "ctx", None), check_vma=False
    )
```

```python
import functools
import math

import jax
import jax.numpy as jnp
import numpy as np
from jax import lax
from jax.experimental import pallas as pl
from jax.experimental.pallas import tpu as pltpu
from jax.sharding import PartitionSpec as P

QUERY_HEADS = 16
KEY_VALUE_HEADS = 4
HEAD_SIZE = 128
GROUP = QUERY_HEADS // KEY_VALUE_HEADS
GROUP_WIDTH = GROUP * HEAD_SIZE
PAIR_WIDTH = 2 * HEAD_SIZE
MASKED = -1e30
NOTE_ROWS = 16

rope_base = 500000.0


def from_behind(block, axis, distance):
    devices = range(lax.axis_size(axis))
    route = [((i - distance) % len(devices), i) for i in devices]
    return lax.ppermute(block, axis, route)


def apply_rotary(key_heads, token_positions):
    half_dim = key_heads.shape[-1] // 2
    frequency = rope_base ** (-jnp.arange(half_dim, dtype=jnp.float32) * 2.0 / key_heads.shape[-1])
    angles = token_positions.astype(jnp.float32)[:, None] * frequency[None, :]
    cosine_part = jnp.cos(angles)[:, None, :]
    sine_part = jnp.sin(angles)[:, None, :]
    lower_half = key_heads[..., :half_dim]
    upper_half = key_heads[..., half_dim:]
    return jnp.concatenate(
        [
            lower_half * cosine_part - upper_half * sine_part,
            upper_half * cosine_part + lower_half * sine_part,
        ],
        axis=-1,
    )


def gathered_everywhere(hidden, queries, key_value_weight, doc_ids, scored):
    count_of_rows = hidden.shape[1]
    first_row = lax.axis_index("ctx") * count_of_rows
    token_positions = first_row + jnp.arange(count_of_rows, dtype=jnp.int32)
    wide = hidden[0].astype(jnp.float32)
    normed = (wide * lax.rsqrt(jnp.mean(wide * wide, axis=-1, keepdims=True) + 1e-05)).astype(
        jnp.bfloat16
    )
    projected_rows = jnp.dot(normed, key_value_weight[0], preferred_element_type=jnp.float32)
    key_value_width = KEY_VALUE_HEADS * HEAD_SIZE
    key_matrix = (
        apply_rotary(
            projected_rows[:, :key_value_width].reshape(count_of_rows, KEY_VALUE_HEADS, HEAD_SIZE),
            token_positions,
        )
        .astype(jnp.bfloat16)
        .reshape(count_of_rows, key_value_width)
    )
    value_matrix = projected_rows[:, key_value_width:].astype(jnp.bfloat16)
    query_head_count = queries[0].reshape(count_of_rows, KEY_VALUE_HEADS, GROUP, HEAD_SIZE)
    sequence_docs = doc_ids[0]
    own_docs = lax.dynamic_slice_in_dim(sequence_docs, first_row, count_of_rows, 0)
    score_scale = 1.0 / math.sqrt(HEAD_SIZE)
    stacked = jnp.concatenate([key_matrix, value_matrix], axis=1)
    collected_rows = lax.all_gather(stacked, "ctx", axis=0, tiled=True)
    sequence_length = collected_rows.shape[0]
    every_key_row = collected_rows[:, :key_value_width].reshape(
        sequence_length, KEY_VALUE_HEADS, HEAD_SIZE
    )
    every_value_row = collected_rows[:, key_value_width:].reshape(
        sequence_length, KEY_VALUE_HEADS, HEAD_SIZE
    )
    head_outputs = []
    for key_value_head in range(KEY_VALUE_HEADS):
        key_part = every_key_row[:, key_value_head : key_value_head + 1]
        key_count = key_part.shape[0]
        scores = (
            jnp.einsum(
                "qhgd,khd->hgqk",
                query_head_count[:, key_value_head : key_value_head + 1],
                key_part,
                preferred_element_type=jnp.float32,
            )
            * score_scale
        )
        key_pos = jnp.arange(key_count, dtype=jnp.int32)
        allowed = (key_pos[None, :] <= token_positions[:, None]) & (
            sequence_docs[None, :] == own_docs[:, None]
        )
        scores = jnp.where(allowed[None, None], scores, jnp.float32(MASKED))
        row_max = jnp.max(scores, axis=-1, keepdims=True)
        expo = jnp.exp(scores - row_max)
        total = jnp.sum(expo, axis=-1)
        weights = expo.astype(jnp.bfloat16)
        summed = jnp.einsum(
            "hgqk,khd->hgqd",
            weights,
            every_value_row[:, key_value_head : key_value_head + 1],
            preferred_element_type=jnp.float32,
        )
        head_outputs.append(summed / total[..., None])
    attended = jnp.transpose(jnp.concatenate(head_outputs, axis=0), (2, 0, 1, 3))
    flat = (
        attended.reshape(count_of_rows, QUERY_HEADS * HEAD_SIZE)
        * scored[0].astype(jnp.float32)[:, None]
    )
    outgoing = flat.astype(jnp.bfloat16)[None]
    return from_behind(outgoing, "phase", 1)


def rotary_table(rows, devices):
    half = HEAD_SIZE // 2
    frequency = (rope_base ** (-np.arange(half) * 2.0 / HEAD_SIZE)).astype(np.float32).astype(np.float64)
    frequency = np.concatenate([frequency, frequency])[None, :]
    angles = np.concatenate([np.arange(rows), rows * np.arange(devices)])[:, None] * frequency
    return jnp.asarray(np.concatenate([np.cos(angles), np.sin(angles)], axis=1), jnp.float32)


def parity():
    return lax.rem(lax.axis_index("ctx") // 2, 2)


def project_kernel(
    cuts,
    hidden,
    weight,
    queries,
    table,
    docs,
    scored,
    mine,
    other,
    swap,
    away,
    packed,
    wide,
    store,
    normed,
    angles,
    doc_row,
    scored_row,
    mine_out,
    other_out,
    swap_out,
    away_out,
    packed_out,
    in_sems,
    weight_sems,
    out_sems,
):
    rows, width = wide.shape[0], packed.shape[1]
    odd = parity()
    own = slice(0, rows)
    sources = [
        (hidden.at[0], wide),
        (table, angles),
        (docs, doc_row),
        (scored, scored_row),
        (
            queries.at[0, :, pl.ds(pl.multiple_of((1 - odd) * GROUP_WIDTH, GROUP_WIDTH), GROUP_WIDTH)],
            swap_out.at[pl.ds(0, rows), pl.ds(PAIR_WIDTH, GROUP_WIDTH)],
        ),
        (queries.at[0, :, pl.ds(width, width)], packed_out.at[pl.ds(0, rows), :]),
    ]
    loads = [
        pltpu.make_async_copy(source, target, in_sems.at[i])
        for i, (source, target) in enumerate(sources)
    ]
    loads[0].start()
    copies = []
    for i, (start, stop) in enumerate(cuts):
        span = pl.ds(start, stop - start)
        copies.append(
            pltpu.make_async_copy(weight.at[0, span, :], store.at[span, :], weight_sems.at[i])
        )
    for copy in copies[:2]:
        copy.start()
    for load in loads[1:]:
        load.start()
    results = [
        pltpu.make_async_copy(source, target, out_sems.at[i])
        for i, (source, target) in enumerate(
            (
                (swap_out, swap),
                (away_out, away),
                (mine_out, mine),
                (other_out, other),
                (packed_out, packed),
            )
        )
    ]
    loads[0].wait()
    for copy in copies[2:3]:
        copy.start()
    values = wide[...].astype(jnp.float32)
    scale = lax.rsqrt(jnp.mean(values * values, axis=-1, keepdims=True) + 1e-05)
    normed[...] = (values * scale).astype(jnp.bfloat16)
    for load in loads[1:]:
        load.wait()
    marks = jnp.concatenate([scored_row[...]] * (width // rows), axis=1)
    notes = [doc_row[...], marks, jnp.zeros((NOTE_ROWS - 2, width), jnp.int32)]
    notes = jnp.concatenate(notes, axis=0).astype(jnp.float32).astype(jnp.bfloat16)
    packed_out[rows:, :] = notes
    swap_out[rows:, :] = notes[:, : swap.shape[1]]
    results[4].start()
    base = angles[pl.ds(rows + lax.axis_index("ctx"), 1), :]
    base_cosine, base_sine = base[:, :HEAD_SIZE], base[:, HEAD_SIZE:]
    cosine, sine = angles[own, :HEAD_SIZE], angles[own, HEAD_SIZE:]
    cosine, sine = (
        cosine * base_cosine - sine * base_sine,
        sine * base_cosine + cosine * base_sine,
    )
    sine = jnp.where(lax.broadcasted_iota(jnp.int32, sine.shape, 1) < HEAD_SIZE // 2, -sine, sine)
    total = None
    for i, (start, stop) in enumerate(cuts):
        copies[i].wait()
        if i + 3 < len(copies):
            copies[i + 3].start()
        part = jnp.dot(
            normed[:, start:stop], store[start:stop, :], preferred_element_type=jnp.float32
        )
        total = part if total is None else total + part
    pairs = []
    for head in range(KEY_VALUE_HEADS):
        key = total[:, head * HEAD_SIZE : (head + 1) * HEAD_SIZE]
        key = key * cosine + pltpu.roll(key, HEAD_SIZE // 2, 1) * sine
        at = (KEY_VALUE_HEADS + head) * HEAD_SIZE
        value = total[:, at : at + HEAD_SIZE]
        pairs.append(jnp.concatenate([key, value], axis=1).astype(jnp.bfloat16))
    for u in range(2):

        @pl.when(odd == u)
        def _():
            mine_out[...] = pairs[u]
            other_out[...] = pairs[1 - u]
            swap_out[own, :PAIR_WIDTH] = pairs[1 - u]

    away_out[:, :PAIR_WIDTH] = pairs[2]
    away_out[:, PAIR_WIDTH:] = pairs[3]
    for result in results[:4]:
        result.start()
    for result in results:
        result.wait()


def project(hidden, weight, queries, docs, scored):
    rows, width = hidden.shape[1], hidden.shape[2]
    columns = weight.shape[2]
    edges = [width * x // 16 for x in [0, 5, 10, 14, 16]]
    cuts = tuple(zip(edges[:-1], edges[1:]))
    table = rotary_table(rows, docs.shape[1] // rows)
    hbm = pl.BlockSpec(memory_space=pltpu.HBM)
    shapes = [
        (rows, PAIR_WIDTH),
        (rows, PAIR_WIDTH),
        (rows + NOTE_ROWS, PAIR_WIDTH + GROUP_WIDTH),
        (rows, 2 * PAIR_WIDTH),
        (rows + NOTE_ROWS, 2 * GROUP_WIDTH),
    ]
    return pl.pallas_call(
        functools.partial(project_kernel, cuts),
        out_shape=[jax.ShapeDtypeStruct(shape, jnp.bfloat16) for shape in shapes],
        in_specs=[hbm] * 6,
        out_specs=[hbm] * 5,
        scratch_shapes=[
            pltpu.VMEM((rows, width), jnp.bfloat16),
            pltpu.VMEM((width, columns), jnp.bfloat16),
            pltpu.VMEM((rows, width), jnp.bfloat16),
            pltpu.VMEM(table.shape, jnp.float32),
            pltpu.VMEM(docs.shape, jnp.int32),
            pltpu.VMEM(scored.shape, jnp.int32),
        ]
        + [pltpu.VMEM(shape, jnp.bfloat16) for shape in shapes]
        + [
            pltpu.SemaphoreType.DMA((6,)),
            pltpu.SemaphoreType.DMA((len(cuts),)),
            pltpu.SemaphoreType.DMA((5,)),
        ],
        compiler_params=pltpu.CompilerParams(vmem_limit_bytes=63 * 2**20),
        cost_estimate=pl.CostEstimate(flops=0, bytes_accessed=0, transcendentals=0),
        name="project",
    )(hidden, weight, queries, table, docs, scored)


def attended(q, keys, values, bias, factor):
    scores = jnp.concatenate(
        [
            lax.dot_general(q, k, (((1,), (1,)), ((), ())), preferred_element_type=jnp.float32)
            for k in keys
        ],
        axis=1,
    )
    scores = scores + bias
    row_max = jnp.max(scores, axis=-1, keepdims=True)
    expo = jnp.exp2((scores - row_max) * factor)
    total = jnp.sum(expo, axis=-1, keepdims=True)
    weights = expo.astype(jnp.bfloat16)
    summed, at = None, 0
    for value in values:
        part = jnp.dot(
            weights[:, at : at + value.shape[0]], value, preferred_element_type=jnp.float32
        )
        summed = part if summed is None else summed + part
        at += value.shape[0]
    return summed / total


def attend_body(q, kvs, doc_row, kept, bias, put):
    rows = q.shape[0]
    place = lax.axis_index("ctx")
    chip, core = place // 2, lax.rem(place, 2)
    cores = (core, 1 - core)

    def docs_of(device):
        row = doc_row(pl.ds(pl.multiple_of(device * rows, rows), rows))
        return jnp.broadcast_to(row.astype(jnp.float32), (rows, rows))

    query_docs = docs_of(place).T
    for back in range(4):
        for b in range(2):
            block = chip - back
            key_docs = docs_of(2 * jnp.maximum(block, 0) + cores[b])
            allowed = query_docs == jnp.where(block >= 0, key_docs, -1.0)
            if back == 0:
                row_at = lax.broadcasted_iota(jnp.int32, (rows, rows), 0)
                key_at = lax.broadcasted_iota(jnp.int32, (rows, rows), 1)
                allowed &= core * rows + row_at >= cores[b] * rows + key_at
            at = (2 * back + b) * rows
            bias[:, at : at + rows] = jnp.where(allowed, 0.0, MASKED)

    kept_rows = jnp.broadcast_to(kept, (rows, rows)).T[:, :1]
    factor = math.log2(math.e) / math.sqrt(HEAD_SIZE)

    def heads(count):
        for head in range(2):
            keys, values = [
                [
                    jnp.concatenate(
                        [kvs[2 * back + b][:, at : at + HEAD_SIZE] for b in range(2)], axis=0
                    )
                    for back in range(count)
                ]
                for at in (head * PAIR_WIDTH, head * PAIR_WIDTH + HEAD_SIZE)
            ]
            for half in range(GROUP // 2):
                at = [(head * GROUP + 2 * half + i) * HEAD_SIZE for i in range(2)]
                pair = jnp.concatenate([q[:, x : x + HEAD_SIZE] for x in at], axis=0)
                mask = bias[:, : 2 * count * rows]
                mask = jnp.concatenate([mask, mask], axis=0)
                result = attended(pair, keys, values, mask, factor)
                for i in range(2):
                    part = result[i * rows : (i + 1) * rows] * kept_rows
                    put(at[i], part.astype(jnp.bfloat16))

    for last in range(4):
        pl.when(chip == last)(functools.partial(heads, last + 1))


def attend_home_kernel(
    queries, swap, mine, mine_x, near_x, far, far_x, beyond, beyond_x, docs, scored, out_own, out_other, bias
):
    rows = queries.shape[1]
    place = lax.axis_index("ctx")
    chip, core = place // 2, lax.rem(place, 2)
    partner = place + 2 - 4 * lax.rem(chip, 2)
    behind = place - 4
    crossed = 2 * (3 - chip) + core
    far_off = chip >= 2

    def other_core(device):
        return device + 1 - 2 * lax.rem(device, 2)

    def docs_of(device):
        start = pl.multiple_of(device * rows, rows)
        return jnp.broadcast_to(docs[:, pl.ds(start, rows)].astype(jnp.float32), (rows, rows))

    row_at = lax.broadcasted_iota(jnp.int32, (rows, rows), 0)
    key_at = lax.broadcasted_iota(jnp.int32, (rows, rows), 1)
    sources = []
    for device in (place, partner, behind, crossed):
        device = jnp.where(far_off, device, lax.rem(device + 8, 8))
        sources += [device, other_core(device)]
    query_docs = [docs_of(place).T, docs_of(partner).T]
    for k, device in enumerate(sources):
        key_docs = docs_of(device)
        if k >= 4:
            key_docs = jnp.where(far_off, key_docs, -1.0)
        for a, asker in enumerate((place, partner)):
            allowed = query_docs[a] == key_docs
            if k < 4:
                allowed &= asker * rows + row_at >= device * rows + key_at
            bias[a * rows : (a + 1) * rows, k * rows : (k + 1) * rows] = jnp.where(
                allowed, 0.0, MASKED
            )

    def blocks(at):
        cut = slice(at, at + HEAD_SIZE)
        return [
            jnp.concatenate([one[:rows, cut], twin[:, cut]], axis=0)
            for one, twin in ((mine, mine_x), (swap, near_x), (far, far_x), (beyond, beyond_x))
        ]

    kept = jnp.concatenate(
        [
            jnp.broadcast_to(row, (rows, rows)).T[:, :1]
            for row in (
                scored[...].astype(jnp.float32),
                swap[rows:, :rows].astype(jnp.float32)[1:2],
            )
        ],
        axis=0,
    )
    factor = math.log2(math.e) / math.sqrt(HEAD_SIZE)

    def heads(count):
        keys, values = blocks(0)[:count], blocks(HEAD_SIZE)[:count]
        for head in range(GROUP):
            at = head * HEAD_SIZE
            asked = swap[:rows, PAIR_WIDTH + at : PAIR_WIDTH + at + HEAD_SIZE]
            q = jnp.concatenate([queries[0, :, at : at + HEAD_SIZE], asked], axis=0)
            result = attended(q, keys, values, bias[:, : 2 * count * rows], factor)
            result = (result * kept).astype(jnp.bfloat16)
            out_own[:, at : at + HEAD_SIZE] = result[:rows]
            out_other[:, at : at + HEAD_SIZE] = result[rows:]

    pl.when(far_off)(lambda: heads(4))
    pl.when(jnp.logical_not(far_off))(lambda: heads(2))


class Halves:
    def __init__(self, first, second):
        self.refs = (first, second)
        self.width = first.shape[1]

    def __getitem__(self, index):
        rows, columns = index
        start = columns.start % self.width
        ref = self.refs[columns.start // self.width]
        return ref[rows, start : start + columns.stop - columns.start]


def attend_relayed_kernel(packed, *refs):
    kvs, (out, bias) = refs[:10], refs[10:]
    kvs = kvs[:5] + (Halves(*kvs[5:7]), kvs[7], Halves(*kvs[8:]))
    rows = out.shape[0]
    kept = packed[rows : rows + NOTE_ROWS, :rows].astype(jnp.float32)[1:2]

    def doc_row(at):
        return packed[rows : rows + NOTE_ROWS, at].astype(jnp.float32)[:1]

    def put(at, value):
        out[:, at : at + HEAD_SIZE] = value

    attend_body(packed.at[pl.ds(0, rows), :], kvs, doc_row, kept, bias, put)


def attend_cost(rows, flops):
    return dict(
        scratch_shapes=[pltpu.VMEM((rows, 8 * rows), jnp.float32)],
        compiler_params=pltpu.CompilerParams(vmem_limit_bytes=32 * 2**20),
        cost_estimate=pl.CostEstimate(flops=flops, bytes_accessed=0, transcendentals=0),
    )


def attend_home(queries, *rest):
    rows = queries.shape[1]
    out = jax.ShapeDtypeStruct((rows, GROUP_WIDTH), jnp.bfloat16)

    def whole(array):
        return pl.BlockSpec(array.shape, lambda i: (0,) * array.ndim)

    cost = attend_cost(rows, HOME_FLOPS)
    cost["scratch_shapes"] = [pltpu.VMEM((2 * rows, 8 * rows), jnp.float32)]
    return pl.pallas_call(
        attend_home_kernel,
        grid=(1,),
        out_shape=(out, out),
        in_specs=[pl.BlockSpec((1, rows, GROUP_WIDTH), lambda i: (0, 0, parity()))]
        + [whole(x) for x in rest],
        out_specs=(pl.BlockSpec((rows, GROUP_WIDTH), lambda i: (0, 0)),) * 2,
        name="attend_home",
        **cost,
    )(queries, *rest)


def attend_relayed(packed, kvs):
    rows, width = kvs[0].shape[0], packed.shape[1]
    vmem = pl.BlockSpec(memory_space=pltpu.VMEM)
    return pl.pallas_call(
        attend_relayed_kernel,
        out_shape=jax.ShapeDtypeStruct((rows, width), jnp.bfloat16),
        in_specs=[vmem] * 11,
        out_specs=vmem,
        name="attend_relayed",
        **attend_cost(rows, RELAYED_FLOPS),
    )(packed, *kvs)


def send(block, route):
    pairs = [(2 * a + core, 2 * b + core) for a, b in route for core in range(2)]
    return lax.ppermute(block, "ctx", pairs)


def across(block):
    return lax.ppermute(block, "ctx", [(i, i ^ 1) for i in range(lax.axis_size("ctx"))])


def onward(block, change=0):
    sections, count = lax.axis_size("phase"), lax.axis_size("ctx")
    route = [
        (p * count + c, (p + 1) % sections * count + (c ^ change))
        for p in range(sections)
        for c in range(count)
    ]
    return lax.ppermute(block, ("phase", "ctx"), route)


HOME_FLOPS = int(1.9 * 10**9)
RELAYED_FLOPS = 0


def after(block, *others):
    return lax.optimization_barrier((block,) + others)[0]


def across_halves(block):
    half = block.shape[1] // 2
    return across(block[:, :half]), across(block[:, half:])


def paired(hidden, queries, key_value_weight, doc_ids, scored):
    mine, other, swap, away, packed = project(hidden, key_value_weight, queries, doc_ids, scored)
    away = onward(away)
    swap = send(swap, ((0, 1), (1, 0), (2, 3), (3, 2)))
    far = send(mine, ((0, 2), (1, 3)))
    beyond = send(other, ((0, 3), (1, 2)))
    packed = onward(packed)
    away_1 = send(away, ((0, 1), (1, 2), (2, 3)))
    away_2 = send(away_1, ((1, 2), (2, 3)))
    away_3 = send(away_1, ((1, 3),))
    mine_x = across(mine)
    own, partners = attend_home(
        queries,
        swap,
        across(mine_x),
        mine_x,
        across(swap[: mine.shape[0], :PAIR_WIDTH]),
        far,
        across(far),
        beyond,
        across(beyond),
        doc_ids,
        scored,
    )
    own, partners = onward(own), onward(partners, 2)
    away = [away, across(away), away_1, across(after(away_1, packed))] + [
        x for block in (away_2, away_3) for x in (block, *across_halves(block))
    ]
    last = attend_relayed(packed, away)
    crossed = jnp.concatenate([partners, own, last], axis=1)
    straight = jnp.concatenate([own, partners, last], axis=1)
    return jnp.where(parity() == 0, straight, crossed)[None]


def solution(mesh):
    placed = (
        P("phase", "ctx", None),
        P("phase", "ctx", None),
        P("phase", None, None),
        P("phase", None),
        P("phase", "ctx"),
    )
    plan = paired if mesh.shape["ctx"] == 8 else gathered_everywhere
    return jax.shard_map(
        plan, mesh=mesh, in_specs=placed, out_specs=P("phase", "ctx", None), check_vma=False
    )
```

```python
import functools
import math

import jax
import jax.numpy as jnp
import numpy as np
from jax import lax
from jax.experimental import pallas as pl
from jax.experimental.pallas import tpu as pltpu
from jax.sharding import PartitionSpec as P

QUERY_HEADS = 16
KEY_VALUE_HEADS = 4
HEAD_SIZE = 128
GROUP = QUERY_HEADS // KEY_VALUE_HEADS
GROUP_WIDTH = GROUP * HEAD_SIZE
PAIR_WIDTH = 2 * HEAD_SIZE
MASKED = -1e30
NOTE_ROWS = 16

rope_base = 500000.0


def from_behind(block, axis, distance):
    devices = range(lax.axis_size(axis))
    route = [((i - distance) % len(devices), i) for i in devices]
    return lax.ppermute(block, axis, route)


def apply_rotary(key_heads, token_positions):
    half_dim = key_heads.shape[-1] // 2
    frequency = rope_base ** (-jnp.arange(half_dim, dtype=jnp.float32) * 2.0 / key_heads.shape[-1])
    angles = token_positions.astype(jnp.float32)[:, None] * frequency[None, :]
    cosine_part = jnp.cos(angles)[:, None, :]
    sine_part = jnp.sin(angles)[:, None, :]
    lower_half = key_heads[..., :half_dim]
    upper_half = key_heads[..., half_dim:]
    return jnp.concatenate(
        [
            lower_half * cosine_part - upper_half * sine_part,
            upper_half * cosine_part + lower_half * sine_part,
        ],
        axis=-1,
    )


def gathered_everywhere(hidden, queries, key_value_weight, doc_ids, scored):
    count_of_rows = hidden.shape[1]
    first_row = lax.axis_index("ctx") * count_of_rows
    token_positions = first_row + jnp.arange(count_of_rows, dtype=jnp.int32)
    wide = hidden[0].astype(jnp.float32)
    normed = (wide * lax.rsqrt(jnp.mean(wide * wide, axis=-1, keepdims=True) + 1e-05)).astype(
        jnp.bfloat16
    )
    projected_rows = jnp.dot(normed, key_value_weight[0], preferred_element_type=jnp.float32)
    key_value_width = KEY_VALUE_HEADS * HEAD_SIZE
    key_matrix = (
        apply_rotary(
            projected_rows[:, :key_value_width].reshape(count_of_rows, KEY_VALUE_HEADS, HEAD_SIZE),
            token_positions,
        )
        .astype(jnp.bfloat16)
        .reshape(count_of_rows, key_value_width)
    )
    value_matrix = projected_rows[:, key_value_width:].astype(jnp.bfloat16)
    query_head_count = queries[0].reshape(count_of_rows, KEY_VALUE_HEADS, GROUP, HEAD_SIZE)
    sequence_docs = doc_ids[0]
    own_docs = lax.dynamic_slice_in_dim(sequence_docs, first_row, count_of_rows, 0)
    score_scale = 1.0 / math.sqrt(HEAD_SIZE)
    stacked = jnp.concatenate([key_matrix, value_matrix], axis=1)
    collected_rows = lax.all_gather(stacked, "ctx", axis=0, tiled=True)
    sequence_length = collected_rows.shape[0]
    every_key_row = collected_rows[:, :key_value_width].reshape(
        sequence_length, KEY_VALUE_HEADS, HEAD_SIZE
    )
    every_value_row = collected_rows[:, key_value_width:].reshape(
        sequence_length, KEY_VALUE_HEADS, HEAD_SIZE
    )
    head_outputs = []
    for key_value_head in range(KEY_VALUE_HEADS):
        key_part = every_key_row[:, key_value_head : key_value_head + 1]
        key_count = key_part.shape[0]
        scores = (
            jnp.einsum(
                "qhgd,khd->hgqk",
                query_head_count[:, key_value_head : key_value_head + 1],
                key_part,
                preferred_element_type=jnp.float32,
            )
            * score_scale
        )
        key_pos = jnp.arange(key_count, dtype=jnp.int32)
        allowed = (key_pos[None, :] <= token_positions[:, None]) & (
            sequence_docs[None, :] == own_docs[:, None]
        )
        scores = jnp.where(allowed[None, None], scores, jnp.float32(MASKED))
        row_max = jnp.max(scores, axis=-1, keepdims=True)
        expo = jnp.exp(scores - row_max)
        total = jnp.sum(expo, axis=-1)
        weights = expo.astype(jnp.bfloat16)
        summed = jnp.einsum(
            "hgqk,khd->hgqd",
            weights,
            every_value_row[:, key_value_head : key_value_head + 1],
            preferred_element_type=jnp.float32,
        )
        head_outputs.append(summed / total[..., None])
    attended = jnp.transpose(jnp.concatenate(head_outputs, axis=0), (2, 0, 1, 3))
    flat = (
        attended.reshape(count_of_rows, QUERY_HEADS * HEAD_SIZE)
        * scored[0].astype(jnp.float32)[:, None]
    )
    outgoing = flat.astype(jnp.bfloat16)[None]
    return from_behind(outgoing, "phase", 1)


def rotary_table(rows, devices):
    half = HEAD_SIZE // 2
    frequency = (rope_base ** (-np.arange(half) * 2.0 / HEAD_SIZE)).astype(np.float32).astype(np.float64)
    frequency = np.concatenate([frequency, frequency])[None, :]
    angles = np.concatenate([np.arange(rows), rows * np.arange(devices)])[:, None] * frequency
    return jnp.asarray(np.concatenate([np.cos(angles), np.sin(angles)], axis=1), jnp.float32)


def parity():
    return lax.rem(lax.axis_index("ctx") // 2, 2)


def project_kernel(
    cuts,
    hidden,
    weight,
    queries,
    table,
    docs,
    scored,
    mine,
    other,
    swap,
    away,
    packed,
    wide,
    store,
    normed,
    angles,
    doc_row,
    scored_row,
    mine_out,
    other_out,
    swap_out,
    away_out,
    packed_out,
    in_sems,
    weight_sems,
    out_sems,
):
    rows, width = wide.shape[0], packed.shape[1]
    odd = parity()
    own = slice(0, rows)
    sources = [
        (hidden.at[0], wide),
        (table, angles),
        (docs, doc_row),
        (scored, scored_row),
        (
            queries.at[0, :, pl.ds(pl.multiple_of((1 - odd) * GROUP_WIDTH, GROUP_WIDTH), GROUP_WIDTH)],
            swap_out.at[pl.ds(0, rows), pl.ds(PAIR_WIDTH, GROUP_WIDTH)],
        ),
        (queries.at[0, :, pl.ds(width, width)], packed_out.at[pl.ds(0, rows), :]),
    ]
    loads = [
        pltpu.make_async_copy(source, target, in_sems.at[i])
        for i, (source, target) in enumerate(sources)
    ]
    loads[0].start()
    copies = []
    for i, (start, stop) in enumerate(cuts):
        span = pl.ds(start, stop - start)
        copies.append(
            pltpu.make_async_copy(weight.at[0, span, :], store.at[span, :], weight_sems.at[i])
        )
    for copy in copies[:2]:
        copy.start()
    for load in loads[1:]:
        load.start()
    results = [
        pltpu.make_async_copy(source, target, out_sems.at[i])
        for i, (source, target) in enumerate(
            (
                (swap_out, swap),
                (away_out, away),
                (mine_out, mine),
                (other_out, other),
                (packed_out, packed),
            )
        )
    ]
    loads[0].wait()
    for copy in copies[2:3]:
        copy.start()
    values = wide[...].astype(jnp.float32)
    scale = lax.rsqrt(jnp.mean(values * values, axis=-1, keepdims=True) + 1e-05)
    normed[...] = (values * scale).astype(jnp.bfloat16)
    for load in loads[1:]:
        load.wait()
    marks = jnp.concatenate([scored_row[...]] * (width // rows), axis=1)
    notes = [doc_row[...], marks, jnp.zeros((NOTE_ROWS - 2, width), jnp.int32)]
    notes = jnp.concatenate(notes, axis=0).astype(jnp.float32).astype(jnp.bfloat16)
    packed_out[rows:, :] = notes
    swap_out[rows:, :] = notes[:, : swap.shape[1]]
    results[4].start()
    base = angles[pl.ds(rows + lax.axis_index("ctx"), 1), :]
    base_cosine, base_sine = base[:, :HEAD_SIZE], base[:, HEAD_SIZE:]
    cosine, sine = angles[own, :HEAD_SIZE], angles[own, HEAD_SIZE:]
    cosine, sine = (
        cosine * base_cosine - sine * base_sine,
        sine * base_cosine + cosine * base_sine,
    )
    sine = jnp.where(lax.broadcasted_iota(jnp.int32, sine.shape, 1) < HEAD_SIZE // 2, -sine, sine)
    total = None
    for i, (start, stop) in enumerate(cuts):
        copies[i].wait()
        if i + 3 < len(copies):
            copies[i + 3].start()
        part = jnp.dot(
            normed[:, start:stop], store[start:stop, :], preferred_element_type=jnp.float32
        )
        total = part if total is None else total + part
    pairs = []
    for head in range(KEY_VALUE_HEADS):
        key = total[:, head * HEAD_SIZE : (head + 1) * HEAD_SIZE]
        key = key * cosine + pltpu.roll(key, HEAD_SIZE // 2, 1) * sine
        at = (KEY_VALUE_HEADS + head) * HEAD_SIZE
        value = total[:, at : at + HEAD_SIZE]
        pairs.append(jnp.concatenate([key, value], axis=1).astype(jnp.bfloat16))
    for u in range(2):

        @pl.when(odd == u)
        def _():
            mine_out[...] = pairs[u]
            other_out[...] = pairs[1 - u]
            swap_out[own, :PAIR_WIDTH] = pairs[1 - u]

    away_out[:, :PAIR_WIDTH] = pairs[2]
    away_out[:, PAIR_WIDTH:] = pairs[3]
    for result in results[:4]:
        result.start()
    for result in results:
        result.wait()


def project(hidden, weight, queries, docs, scored):
    rows, width = hidden.shape[1], hidden.shape[2]
    columns = weight.shape[2]
    edges = [width * x // 16 for x in [0, 5, 10, 14, 16]]
    cuts = tuple(zip(edges[:-1], edges[1:]))
    table = rotary_table(rows, docs.shape[1] // rows)
    hbm = pl.BlockSpec(memory_space=pltpu.HBM)
    shapes = [
        (rows, PAIR_WIDTH),
        (rows, PAIR_WIDTH),
        (rows + NOTE_ROWS, PAIR_WIDTH + GROUP_WIDTH),
        (rows, 2 * PAIR_WIDTH),
        (rows + NOTE_ROWS, 2 * GROUP_WIDTH),
    ]
    return pl.pallas_call(
        functools.partial(project_kernel, cuts),
        out_shape=[jax.ShapeDtypeStruct(shape, jnp.bfloat16) for shape in shapes],
        in_specs=[hbm] * 6,
        out_specs=[hbm] * 5,
        scratch_shapes=[
            pltpu.VMEM((rows, width), jnp.bfloat16),
            pltpu.VMEM((width, columns), jnp.bfloat16),
            pltpu.VMEM((rows, width), jnp.bfloat16),
            pltpu.VMEM(table.shape, jnp.float32),
            pltpu.VMEM(docs.shape, jnp.int32),
            pltpu.VMEM(scored.shape, jnp.int32),
        ]
        + [pltpu.VMEM(shape, jnp.bfloat16) for shape in shapes]
        + [
            pltpu.SemaphoreType.DMA((6,)),
            pltpu.SemaphoreType.DMA((len(cuts),)),
            pltpu.SemaphoreType.DMA((5,)),
        ],
        compiler_params=pltpu.CompilerParams(vmem_limit_bytes=63 * 2**20),
        cost_estimate=pl.CostEstimate(flops=0, bytes_accessed=0, transcendentals=0),
        name="project",
    )(hidden, weight, queries, table, docs, scored)


def attended(q, keys, values, bias, factor):
    scores = jnp.concatenate(
        [
            lax.dot_general(q, k, (((1,), (1,)), ((), ())), preferred_element_type=jnp.float32)
            for k in keys
        ],
        axis=1,
    )
    scores = scores + bias
    row_max = jnp.max(scores, axis=-1, keepdims=True)
    expo = jnp.exp2((scores - row_max) * factor)
    total = jnp.sum(expo, axis=-1, keepdims=True)
    weights = expo.astype(jnp.bfloat16)
    summed, at = None, 0
    for value in values:
        part = jnp.dot(
            weights[:, at : at + value.shape[0]], value, preferred_element_type=jnp.float32
        )
        summed = part if summed is None else summed + part
        at += value.shape[0]
    return summed / total


def attend_body(q, kvs, doc_row, kept, bias, put):
    rows = q.shape[0]
    place = lax.axis_index("ctx")
    chip, core = place // 2, lax.rem(place, 2)
    cores = (core, 1 - core)

    def docs_of(device):
        row = doc_row(pl.ds(pl.multiple_of(device * rows, rows), rows))
        return jnp.broadcast_to(row.astype(jnp.float32), (rows, rows))

    query_docs = docs_of(place).T
    for back in range(4):
        for b in range(2):
            block = chip - back
            key_docs = docs_of(2 * jnp.maximum(block, 0) + cores[b])
            allowed = query_docs == jnp.where(block >= 0, key_docs, -1.0)
            if back == 0:
                row_at = lax.broadcasted_iota(jnp.int32, (rows, rows), 0)
                key_at = lax.broadcasted_iota(jnp.int32, (rows, rows), 1)
                allowed &= core * rows + row_at >= cores[b] * rows + key_at
            at = (2 * back + b) * rows
            bias[:, at : at + rows] = jnp.where(allowed, 0.0, MASKED)

    kept_rows = jnp.broadcast_to(kept, (rows, rows)).T[:, :1]
    factor = math.log2(math.e) / math.sqrt(HEAD_SIZE)

    def heads(count):
        for head in range(2):
            keys, values = [
                [
                    jnp.concatenate(
                        [kvs[2 * back + b][:, at : at + HEAD_SIZE] for b in range(2)], axis=0
                    )
                    for back in range(count)
                ]
                for at in (head * PAIR_WIDTH, head * PAIR_WIDTH + HEAD_SIZE)
            ]
            for half in range(GROUP // 2):
                at = [(head * GROUP + 2 * half + i) * HEAD_SIZE for i in range(2)]
                pair = jnp.concatenate([q[:, x : x + HEAD_SIZE] for x in at], axis=0)
                mask = bias[:, : 2 * count * rows]
                mask = jnp.concatenate([mask, mask], axis=0)
                result = attended(pair, keys, values, mask, factor)
                for i in range(2):
                    part = result[i * rows : (i + 1) * rows] * kept_rows
                    put(at[i], part.astype(jnp.bfloat16))

    for last in range(4):
        pl.when(chip == last)(functools.partial(heads, last + 1))


def attend_home_kernel(
    queries, swap, mine, mine_x, near_x, far, far_x, beyond, beyond_x, docs, scored, out_own, out_other, bias
):
    rows = queries.shape[1]
    place = lax.axis_index("ctx")
    chip, core = place // 2, lax.rem(place, 2)
    partner = place + 2 - 4 * lax.rem(chip, 2)
    behind = place - 4
    crossed = 2 * (3 - chip) + core
    far_off = chip >= 2

    def other_core(device):
        return device + 1 - 2 * lax.rem(device, 2)

    def docs_of(device):
        start = pl.multiple_of(device * rows, rows)
        return jnp.broadcast_to(docs[:, pl.ds(start, rows)].astype(jnp.float32), (rows, rows))

    row_at = lax.broadcasted_iota(jnp.int32, (rows, rows), 0)
    key_at = lax.broadcasted_iota(jnp.int32, (rows, rows), 1)
    sources = []
    for device in (place, partner, behind, crossed):
        device = jnp.where(far_off, device, lax.rem(device + 8, 8))
        sources += [device, other_core(device)]
    query_docs = [docs_of(place).T, docs_of(partner).T]
    for k, device in enumerate(sources):
        key_docs = docs_of(device)
        if k >= 4:
            key_docs = jnp.where(far_off, key_docs, -1.0)
        for a, asker in enumerate((place, partner)):
            allowed = query_docs[a] == key_docs
            if k < 4:
                allowed &= asker * rows + row_at >= device * rows + key_at
            bias[a * rows : (a + 1) * rows, k * rows : (k + 1) * rows] = jnp.where(
                allowed, 0.0, MASKED
            )

    def blocks(at):
        cut = slice(at, at + HEAD_SIZE)
        return [
            jnp.concatenate([one[:rows, cut], twin[:, cut]], axis=0)
            for one, twin in ((mine, mine_x), (swap, near_x), (far, far_x), (beyond, beyond_x))
        ]

    kept = jnp.concatenate(
        [
            jnp.broadcast_to(row, (rows, rows)).T[:, :1]
            for row in (
                scored[...].astype(jnp.float32),
                swap[rows:, :rows].astype(jnp.float32)[1:2],
            )
        ],
        axis=0,
    )
    factor = math.log2(math.e) / math.sqrt(HEAD_SIZE)

    def heads(count):
        keys, values = blocks(0)[:count], blocks(HEAD_SIZE)[:count]
        for head in range(GROUP):
            at = head * HEAD_SIZE
            asked = swap[:rows, PAIR_WIDTH + at : PAIR_WIDTH + at + HEAD_SIZE]
            q = jnp.concatenate([queries[0, :, at : at + HEAD_SIZE], asked], axis=0)
            result = attended(q, keys, values, bias[:, : 2 * count * rows], factor)
            result = (result * kept).astype(jnp.bfloat16)
            out_own[:, at : at + HEAD_SIZE] = result[:rows]
            out_other[:, at : at + HEAD_SIZE] = result[rows:]

    pl.when(far_off)(lambda: heads(4))
    pl.when(jnp.logical_not(far_off))(lambda: heads(2))


class Halves:
    def __init__(self, first, second):
        self.refs = (first, second)
        self.width = first.shape[1]

    def __getitem__(self, index):
        rows, columns = index
        start = columns.start % self.width
        ref = self.refs[columns.start // self.width]
        return ref[rows, start : start + columns.stop - columns.start]


def attend_relayed_kernel(packed, *refs):
    kvs, (out, bias) = refs[:9], refs[9:]
    kvs = kvs[:5] + (Halves(*kvs[5:7]), *kvs[7:])
    rows = out.shape[0]
    kept = packed[rows : rows + NOTE_ROWS, :rows].astype(jnp.float32)[1:2]

    def doc_row(at):
        return packed[rows : rows + NOTE_ROWS, at].astype(jnp.float32)[:1]

    def put(at, value):
        out[:, at : at + HEAD_SIZE] = value

    attend_body(packed.at[pl.ds(0, rows), :], kvs, doc_row, kept, bias, put)


def attend_cost(rows, flops):
    return dict(
        scratch_shapes=[pltpu.VMEM((rows, 8 * rows), jnp.float32)],
        compiler_params=pltpu.CompilerParams(vmem_limit_bytes=32 * 2**20),
        cost_estimate=pl.CostEstimate(flops=flops, bytes_accessed=0, transcendentals=0),
    )


def attend_home(queries, *rest):
    rows = queries.shape[1]
    out = jax.ShapeDtypeStruct((rows, GROUP_WIDTH), jnp.bfloat16)

    def whole(array):
        return pl.BlockSpec(array.shape, lambda i: (0,) * array.ndim)

    cost = attend_cost(rows, HOME_FLOPS)
    cost["scratch_shapes"] = [pltpu.VMEM((2 * rows, 8 * rows), jnp.float32)]
    return pl.pallas_call(
        attend_home_kernel,
        grid=(1,),
        out_shape=(out, out),
        in_specs=[pl.BlockSpec((1, rows, GROUP_WIDTH), lambda i: (0, 0, parity()))]
        + [whole(x) for x in rest],
        out_specs=(pl.BlockSpec((rows, GROUP_WIDTH), lambda i: (0, 0)),) * 2,
        name="attend_home",
        **cost,
    )(queries, *rest)


def attend_relayed(packed, kvs):
    rows, width = kvs[0].shape[0], packed.shape[1]
    vmem = pl.BlockSpec(memory_space=pltpu.VMEM)
    return pl.pallas_call(
        attend_relayed_kernel,
        out_shape=jax.ShapeDtypeStruct((rows, width), jnp.bfloat16),
        in_specs=[vmem] * 10,
        out_specs=vmem,
        name="attend_relayed",
        **attend_cost(rows, RELAYED_FLOPS),
    )(packed, *kvs)


def send(block, route):
    pairs = [(2 * a + core, 2 * b + core) for a, b in route for core in range(2)]
    return lax.ppermute(block, "ctx", pairs)


def across(block):
    return lax.ppermute(block, "ctx", [(i, i ^ 1) for i in range(lax.axis_size("ctx"))])


def onward(block, change=0):
    sections, count = lax.axis_size("phase"), lax.axis_size("ctx")
    route = [
        (p * count + c, (p + 1) % sections * count + (c ^ change))
        for p in range(sections)
        for c in range(count)
    ]
    return lax.ppermute(block, ("phase", "ctx"), route)


HOME_FLOPS = int(1.9 * 10**9)
RELAYED_FLOPS = 0


def after(block, *others):
    return lax.optimization_barrier((block,) + others)[0]


def across_halves(block):
    half = block.shape[1] // 2
    return across(block[:, :half]), across(block[:, half:])


def paired(hidden, queries, key_value_weight, doc_ids, scored):
    mine, other, swap, away, packed = project(hidden, key_value_weight, queries, doc_ids, scored)
    away = onward(away)
    swap = send(swap, ((0, 1), (1, 0), (2, 3), (3, 2)))
    far = send(mine, ((0, 2), (1, 3)))
    beyond = send(other, ((0, 3), (1, 2)))
    packed = onward(packed)
    away_1 = send(away, ((0, 1), (1, 2), (2, 3)))
    away_2 = send(away_1, ((1, 2), (2, 3)))
    away_3 = send(away_1, ((1, 3),))
    mine_x = across(mine)
    own, partners = attend_home(
        queries,
        swap,
        across(mine_x),
        mine_x,
        across(swap[: mine.shape[0], :PAIR_WIDTH]),
        far,
        across(far),
        beyond,
        across(beyond),
        doc_ids,
        scored,
    )
    own, partners = onward(own), onward(partners, 2)
    away = [away, across(away), away_1, across(after(away_1, packed)), away_2]
    away += [*across_halves(away_2), away_3, across(away_3)]
    last = attend_relayed(packed, away)
    straight = jnp.concatenate([own, partners, last], axis=1)
    crossed = jnp.concatenate([partners, own, last], axis=1)
    return jnp.where(parity() == 1, crossed, straight)[None]


def solution(mesh):
    placed = (
        P("phase", "ctx", None),
        P("phase", "ctx", None),
        P("phase", None, None),
        P("phase", None),
        P("phase", "ctx"),
    )
    plan = paired if mesh.shape["ctx"] == 8 else gathered_everywhere
    return jax.shard_map(
        plan, mesh=mesh, in_specs=placed, out_specs=P("phase", "ctx", None), check_vma=False
    )
```
